128 devices in a mesh: gy: 16 (over x, z_lo, core), gz: 8 (over y, z_hi).
Axes of the slice: x: 4, y: 4, z: 4 (z_hi: 2, z_lo: 2; z = z_hi * 2 + z_lo), core: 2. Of those that a mesh axis runs over, the one named last changes fastest.
Arguments:
- field: bfloat16 [32, 2, 2048, 2048], P(None, None, 'gy', 'gz'), may hold values from -6 to 6
- spec_weight: bfloat16 [4096, 2048], P(('gy', 'gz')), may hold values from -4 to 4
- point_weight: bfloat16 [32, 32], replicated, may hold values from -1 to 1
- bias: bfloat16 [32], replicated, may hold values from -3 to 3
- cotangent: bfloat16 [32, 2, 2048, 2048], P(None, None, 'gy', 'gz'), may hold values from -16 to 16
Outputs:
- output: bfloat16 [32, 2, 2048, 2048], P(None, None, 'gy', 'gz')
- grad_input: bfloat16 [32, 2, 2048, 2048], P(None, None, 'gy', 'gz')
- grad_spec: float32 [4096, 2048], P(('gy', 'gz'))
- grad_point: float32 [32, 32], replicated
- grad_bias: float32 [32], replicated
The draws below stay inside these ranges and needn't reach their ends.
All inputs are finite; a program needn't handle non-finite values.
Results may differ from the reference program's by a relative error of at most 0.008.
Values may be sent and summed in bfloat16 or wider, within the bound.
A program may use at most 128 MiB of HBM per device.

```python
import math
import jax
import jax.numpy as jnp
from jax import lax

C = 32
Y = 2048
Z = 2048
KY = 64
KZ = 64
X = 2


def draw_cotangent(key, part):
    key = jax.random.fold_in(key, 11)
    first_key = jax.random.fold_in(key, 0)
    ramp = 1.0 + jnp.arange(Y, dtype=jnp.float32)[:, None] / Y + jnp.arange(Z, dtype=jnp.float32)[None, :] / Z
    values = jax.random.truncated_normal(first_key, -4.0, 4.0, (C, X, Y, Z), jnp.float32)
    return (values * ramp).astype(jnp.bfloat16)


def shard_levels(stream_key, extent, cuts, least, largest):
    level = 1.0
    for dim, parts in cuts:
        draws = jax.random.uniform(jax.random.fold_in(jax.random.fold_in(stream_key, 6), dim), (parts,), jnp.float32, least / len(cuts), largest / len(cuts))
        level = level * jnp.repeat(jnp.exp(draws), extent[dim] // parts).reshape((-1,) + (1,) * (len(extent) - 1 - dim))
    return level


def noise(rng, extent, deviation, limit, shards=(), kind=jnp.bfloat16):
    entries = jax.random.normal(rng, extent, jnp.float32) * deviation
    if len(shards) > 0:
        entries = shard_levels(rng, extent, shards, -0.22, 0.18) * entries
    return jnp.clip(entries, min=-limit, max=limit).astype(kind)


def setup_inputs(seed: int = 0) -> dict:
    seeds = jax.random.split(jax.random.key(seed), 6)
    field = noise(seeds[0], (C, X, Y, Z), 1.0, 6.0, ((2, 16), (3, 8)))
    spec_weight = noise(seeds[1], (KY * KZ, 2 * C * C), 1.0, 4.0, ((0, 128),))
    point_weight = noise(seeds[2], (C, C), C ** -0.5, 1.0)
    bias = noise(seeds[3], (C,), 0.5, 3.0)
    cotangent = draw_cotangent(jax.random.fold_in(seeds[5], 71), 0)
    return dict(field=field, spec_weight=spec_weight, point_weight=point_weight, bias=bias, cotangent=cotangent)


highest = lax.Precision.HIGHEST

def wave_table(freq, position, length):
    turns = freq[:, None] * position[None, :] % length
    angle = turns.astype(jnp.float32) * (2.0 * math.pi / length)
    return (jnp.cos(angle), jnp.sin(angle))

def kept_freq(index, length, kept):
    return jnp.where(index < kept // 2, index, length - kept + index)

def tables():
    y_cosine, y_sine = wave_table(kept_freq(jnp.arange(KY, dtype=jnp.int32), Y, KY), jnp.arange(Y, dtype=jnp.int32), Y)
    z_cosine, z_sine = wave_table(jnp.arange(KZ, dtype=jnp.int32), jnp.arange(Z, dtype=jnp.int32), Z)
    return (y_cosine, y_sine, z_cosine, z_sine)

def forward_map(plane):
    y_cosine, y_sine, z_cosine, z_sine = tables()
    scale = 1.0 / math.sqrt(Y * Z)
    z_real = jnp.einsum('cyz,kz->cyk', plane, z_cosine, precision=highest)
    z_imag = -jnp.einsum('cyz,kz->cyk', plane, z_sine, precision=highest)
    real_part = jnp.einsum('jy,cyk->jkc', y_cosine, z_real, precision=highest) + jnp.einsum('jy,cyk->jkc', y_sine, z_imag, precision=highest)
    imag_part = jnp.einsum('jy,cyk->jkc', y_cosine, z_imag, precision=highest) - jnp.einsum('jy,cyk->jkc', y_sine, z_real, precision=highest)
    return (real_part * scale, imag_part * scale)

def inverse_map(real_part, imag_part):
    y_cosine, y_sine, z_cosine, z_sine = tables()
    scale = 2.0 / math.sqrt(Y * Z)
    sum_real = jnp.einsum('jy,jkc->cyk', y_cosine, real_part, precision=highest) - jnp.einsum('jy,jkc->cyk', y_sine, imag_part, precision=highest)
    sum_imag = jnp.einsum('jy,jkc->cyk', y_cosine, imag_part, precision=highest) + jnp.einsum('jy,jkc->cyk', y_sine, real_part, precision=highest)
    grid = jnp.einsum('cyk,kz->cyz', sum_real, z_cosine, precision=highest) - jnp.einsum('cyk,kz->cyz', sum_imag, z_sine, precision=highest)
    return grid * scale

def pre_layer(plane, weights, point, offset):
    real_part, imag_part = forward_map(plane)
    w_real = weights[:, :, 0]
    w_imag = weights[:, :, 1]
    mixed_real = jnp.einsum('jkc,jkco->jko', real_part, w_real, precision=highest) - jnp.einsum('jkc,jkco->jko', imag_part, w_imag, precision=highest)
    mixed_imag = jnp.einsum('jkc,jkco->jko', imag_part, w_real, precision=highest) + jnp.einsum('jkc,jkco->jko', real_part, w_imag, precision=highest)
    spectral = inverse_map(mixed_real, mixed_imag)
    pointwise = jnp.einsum('oi,iyz->oyz', point, plane, precision=highest)
    return spectral + pointwise + offset[:, None, None]

def reference(field, spec_weight, point_weight, bias, cotangent):
    weights = spec_weight.astype(jnp.float32).reshape(KY, KZ, 2, C, C)
    point = point_weight.astype(jnp.float32)
    offset = bias.astype(jnp.float32)

    def one_plane(carry, planes):
        plane_in, plane_cot = planes
        plane_wide = plane_in.astype(jnp.float32)
        pre, pullback = jax.vjp(pre_layer, plane_wide, weights, point, offset)
        result = jax.nn.gelu(pre, approximate=False).astype(jnp.bfloat16)
        slope = 0.5 * (1.0 + jax.scipy.special.erf(pre / math.sqrt(2.0))) + pre * jnp.exp(-0.5 * pre * pre) / math.sqrt(2.0 * math.pi)
        grad_pre = (plane_cot.astype(jnp.float32) * slope).astype(jnp.bfloat16)
        d_plane, d_weights, d_point, d_offset = pullback(grad_pre.astype(jnp.float32))
        carry = (carry[0] + d_weights, carry[1] + d_point, carry[2] + d_offset)
        return (carry, (result, d_plane.astype(jnp.bfloat16)))
    start = (jnp.zeros((KY, KZ, 2, C, C), jnp.float32), jnp.zeros((C, C), jnp.float32), jnp.zeros((C,), jnp.float32))
    sums, stacked = lax.scan(one_plane, start, (jnp.moveaxis(field, 1, 0), jnp.moveaxis(cotangent, 1, 0)))
    output = jnp.moveaxis(stacked[0], 0, 1)
    grad_input = jnp.moveaxis(stacked[1], 0, 1)
    factor = 1.0 / math.sqrt(X * Y * Z)
    grad_spec = sums[0].reshape(KY * KZ, 2 * C * C)
    return (output, grad_input, grad_spec, sums[1] * factor, sums[2] * factor)
```

```python
import functools
import math

import jax
import jax.numpy as jnp
import numpy as np
from jax import lax
from jax.experimental import pallas as pl
from jax.experimental.pallas import tpu as pltpu

P = jax.sharding.PartitionSpec
BF = jnp.bfloat16
F32 = jnp.float32

C = 32
X = 2
Y = 2048
Z = 2048
K = 64
ROWS = 128
COLS = 256
G = 16
NG = ROWS // G

MESH = pl.DeviceIdType.MESH


def row_order():
    order = []
    for core in range(2):
        for cx in range(4):
            for cy in range(4):
                for lo in range(2):
                    order.append(cx * 16 + lo * 8 + core * 4 + cy)
    return np.array(order)


def make_tables():
    j = row_order()
    fy = np.where(j < K // 2, j, Y - K + j)
    y = np.arange(Y)
    ang_y = 2.0 * np.pi * ((fy[:, None] * y[None, :]) % Y) / Y
    z = np.arange(Z)
    ang_z = 2.0 * np.pi * ((np.arange(K)[:, None] * z[None, :]) % Z) / Z
    cy, sy = np.cos(ang_y), np.sin(ang_y)
    cz, sz = np.cos(ang_z), np.sin(ang_z)
    zf = np.concatenate([cz, -sz, -sz, -cz], axis=0)
    zf = zf.reshape(4 * K, Z // COLS, COLS).transpose(1, 0, 2)
    yf = np.stack([cy, sy], axis=0).reshape(2, K, Y // ROWS, ROWS)
    yf = yf.transpose(2, 1, 0, 3).reshape(Y // ROWS, K, 2 * ROWS)
    yi = np.stack([cy, sy], axis=0).reshape(2, K, Y // ROWS, ROWS)
    yi = yi.transpose(2, 0, 3, 1).reshape(Y // ROWS, 2 * ROWS, K)
    bf = lambda a: np.ascontiguousarray(a).astype(jnp.bfloat16)
    scale = 1.0 / math.sqrt(Y * Z)
    return (
        bf(zf.transpose(0, 2, 1)),
        bf(zf),
        bf(yf * scale),
        bf(yi * (2.0 * scale)),
    )


def make_spreads():
    lane = np.arange(C * C)
    rows = np.arange(C)[:, None]
    over_o = (lane[None, :] // C == rows).astype(np.float32)
    over_i = (lane[None, :] % C == rows).astype(np.float32)
    return over_o.astype(jnp.bfloat16), over_i.astype(jnp.bfloat16)


def dot(a, b):
    return jnp.dot(a, b, preferred_element_type=F32)


def dot_nt(a, b):
    return lax.dot_general(a, b, (((1,), (1,)), ((), ())), preferred_element_type=F32)


def split(v):
    hi = v.astype(BF)
    return hi, (v - hi.astype(F32)).astype(BF)


def rows_to_modes(get_rows, yf_ref, wide, part):
    @pl.loop(0, C // 4)
    def _(n):
        for e in range(4):
            c = n * 4 + e
            d = get_rows(c)
            wide[pl.ds(c, K, stride=C), :] = dot(yf_ref[:, :ROWS], d[:, : 2 * K]) + dot(
                yf_ref[:, ROWS:], d[:, 2 * K :]
            )

    @pl.loop(0, 8)
    def _(n):
        at = pl.multiple_of(n * (K * C // 8), K * C // 8)
        part[pl.ds(n * (K // 8), K // 8)] = (
            wide[pl.ds(at, K * C // 8), :].astype(BF).reshape(K // 8, C, 2 * K)
        )


def modes_to_rows(part, yi_ref, wide, spread):
    @pl.loop(0, 8)
    def _(n):
        at = pl.multiple_of(n * (K * C // 8), K * C // 8)
        wide[pl.ds(at, K * C // 8), :] = (
            part[pl.ds(n * (K // 8), K // 8)].astype(F32).reshape(K * C // 8, 2 * K)
        )

    @pl.loop(0, C // 4)
    def _(n):
        for e in range(4):
            c = n * 4 + e
            m = wide[pl.ds(c, K, stride=C), :].astype(BF)
            r = dot(yi_ref[...], m).astype(BF)
            spread[c, :, : 2 * K] = r[:ROWS]
            spread[c, :, 2 * K :] = r[ROWS:]


def first_kernel(field, zf, yf, out, buf, rows, wide, sems):
    copies = [pltpu.make_async_copy(field.at[:, x], buf.at[x], sems.at[x]) for x in range(X)]
    for copy in copies:
        copy.start()
    for x in range(X):
        copies[x].wait()

        @pl.loop(0, C // 2)
        def _(n):
            f = buf[x, pl.ds(n * 2, 2)].reshape(2 * ROWS, COLS)
            rows[pl.ds(n * 2, 2)] = dot(f, zf[...]).astype(BF).reshape(2, ROWS, 4 * K)

        rows_to_modes(lambda c: rows[c], yf, wide, out.at[x])


def places():
    gy, gz = lax.axis_index("gy"), lax.axis_index("gz")
    return dict(x=gy // 4, lo=gy // 2 % 2, core=gy % 2, y=gz // 2, hi=gz % 2)


def device(at, **other):
    at = dict(at, **other)
    return {
        "gy": at["x"] * 4 + at["lo"] * 2 + at["core"],
        "gz": at["y"] * 2 + at["hi"],
    }


def turned(at, axis, step):
    return lax.rem(at[axis] + step, 4)


def z_partners(at):
    return [
        dict(hi=at["hi"], lo=1 - at["lo"]),
        dict(hi=1 - at["hi"], lo=at["lo"]),
        dict(hi=1 - at["hi"], lo=1 - at["lo"]),
    ]


def greet(at):
    barrier = pltpu.get_barrier_semaphore()
    partners = [device(at, core=1 - at["core"])]
    for axis in ("x", "y"):
        partners += [device(at, **{axis: turned(at, axis, s)}) for s in (1, 2, 3)]
    partners += [device(at, **p) for p in z_partners(at)]
    for partner in partners:
        pl.semaphore_signal(barrier, inc=1, device_id=partner, device_id_type=MESH)
    pl.semaphore_wait(barrier, len(partners))


AXES = (("x", "y"), ("y", "x"))


def send(src, dst, sems, n, to):
    send_sem, recv_sem = sems
    copy = pltpu.make_async_remote_copy(
        src_ref=src,
        dst_ref=dst,
        send_sem=send_sem.at[n],
        recv_sem=recv_sem.at[n],
        device_id=to,
        device_id_type=MESH,
    )
    copy.start()
    return copy


def scatter_core(at, p, part, b, sems):
    other = 1 - at["core"]
    return [send(part.at[p, other], b["r1"].at[p], sems, 18 * p, device(at, core=other))]


def scatter_first(at, p, part, b, sems):
    me = at["core"]
    b["s1"][p] = (part[p, me].astype(F32) + b["r1"][p].astype(F32)).astype(BF)
    axis = AXES[p][0]
    copies = []
    for s in (1, 2, 3):
        to = turned(at, axis, s)
        src = b["s1"].at[p, to] if axis == "x" else b["s1"].at[p, :, to]
        copies.append(
            send(src, b["r2"].at[p, s - 1], sems, 18 * p + s, device(at, **{axis: to}))
        )
    return copies


def scatter_second(at, p, part, b, sems):
    axis, second = AXES[p]
    own = b["s1"][p, at["x"]] if axis == "x" else b["s1"][p, :, at["y"]]
    total = own.astype(F32)
    for s in range(3):
        total = total + b["r2"][p, s].astype(F32)
    b["s2"][p] = total.astype(BF)
    copies = []
    for s in (1, 2, 3):
        to = turned(at, second, s)
        copies.append(
            send(
                b["s2"].at[p, to],
                b["r3"].at[p, s - 1],
                sems,
                18 * p + 3 + s,
                device(at, **{second: to}),
            )
        )
    return copies


def scatter_last(at, p, part, b, sems):
    second = AXES[p][1]
    total = b["s2"][p, at[second]].astype(F32)
    for s in range(3):
        total = total + b["r3"][p, s].astype(F32)
    b["s3"][p] = total
    b["s3h"][p] = total.astype(BF)
    copies = []
    for n, to in enumerate(z_partners(at)):
        copies.append(
            send(
                b["s3h"].at[p, to["lo"]],
                b["r4"].at[p, n],
                sems,
                18 * p + 7 + n,
                device(at, **to),
            )
        )
    return copies


def scatter_total(at, p, b):
    total = b["s3"][p, at["lo"]]
    for n in range(3):
        total = total + b["r4"][p, n].astype(F32)
    return total


def gather_first(at, p, modes, sems):
    here = modes.at[p, at["core"], at["x"], at["y"], at["lo"]]
    return [send(here, here, sems, 18 * p + 10, device(at, lo=1 - at["lo"]))]


def gather_second(at, p, modes, sems):
    here = modes.at[p, at["core"], at["x"], at["y"]]
    axis = AXES[p][1]
    return [
        send(here, here, sems, 18 * p + 10 + s, device(at, **{axis: turned(at, axis, s)}))
        for s in (1, 2, 3)
    ]


def gather_third(at, p, modes, sems):
    axis = AXES[p][0]
    if axis == "x":
        here = modes.at[p, at["core"], at["x"]]
    else:
        here = modes.at[p, at["core"], :, at["y"]]
    return [
        send(here, here, sems, 18 * p + 13 + s, device(at, **{axis: turned(at, axis, s)}))
        for s in (1, 2, 3)
    ]


def gather_core(at, p, modes, sems):
    here = modes.at[p, at["core"]]
    return [send(here, here, sems, 18 * p + 17, device(at, core=1 - at["core"]))]


N_SEMS = 36


def exchange_scratch():
    return dict(
        r1=pltpu.VMEM((X, 4, 4, 2, C, 2 * K), BF),
        s1=pltpu.VMEM((X, 4, 4, 2, C, 2 * K), BF),
        r2=pltpu.VMEM((X, 3, 4, 2, C, 2 * K), BF),
        s2=pltpu.VMEM((X, 4, 2, C, 2 * K), BF),
        r3=pltpu.VMEM((X, 3, 2, C, 2 * K), BF),
        s3=pltpu.VMEM((X, 2, C, 2 * K), F32),
        s3h=pltpu.VMEM((X, 2, C, 2 * K), BF),
        r4=pltpu.VMEM((X, 3, C, 2 * K), BF),
        sends=pltpu.SemaphoreType.DMA((N_SEMS,)),
        recvs=pltpu.SemaphoreType.DMA((N_SEMS,)),
    )


def run_scatter(at, part, b, sems, every):
    flight = [scatter_core(at, p, part, b, sems) for p in range(X)]
    every += flight[0] + flight[1]
    for stage in (scatter_first, scatter_second, scatter_last):
        for p in range(X):
            for copy in flight[p]:
                copy.wait_recv()
            flight[p] = stage(at, p, part, b, sems)
            every += flight[p]
    totals = []
    for p in range(X):
        for copy in flight[p]:
            copy.wait_recv()
        totals.append(scatter_total(at, p, b))
    return totals


def run_gather(at, modes, sems, every):
    flight = [gather_first(at, p, modes, sems) for p in range(X)]
    every += flight[0] + flight[1]
    for stage in (gather_second, gather_third, gather_core):
        for p in range(X):
            for copy in flight[p]:
                copy.wait_recv()
            flight[p] = stage(at, p, modes, sems)
            every += flight[p]
    for p in range(X):
        for copy in flight[p]:
            copy.wait_recv()


def widen(v, table):
    hi, lo = split(v)
    return dot(hi, table) + dot(lo, table)


def narrow(v, table):
    hi, lo = split(v)
    return dot_nt(hi, table) + dot_nt(lo, table)


def put_modes(at, p, modes, real, imag):
    block = jnp.concatenate([real, imag], axis=0).T
    modes[p, at["core"], at["x"], at["y"], at["lo"]] = block.astype(BF)


def mix_kernel(part, weights, over_o, over_i, modes, spec, w_all, b, w_sems):
    at = places()
    greet(at)
    sems = (b["sends"], b["recvs"])
    every = []
    hi = at["hi"]
    w_here = pltpu.make_async_copy(weights, w_all.at[hi], w_sems.at[0])
    w_here.start()
    w_there = pltpu.make_async_remote_copy(
        src_ref=weights,
        dst_ref=w_all.at[hi],
        send_sem=w_sems.at[1],
        recv_sem=w_sems.at[2],
        device_id=device(at, hi=1 - hi),
        device_id_type=MESH,
    )
    w_there.start()
    totals = run_scatter(at, part, b, sems, every)
    w_here.wait()
    w_there.wait()
    w = w_all[...].reshape(K, 2 * C * C).astype(F32)
    w_real, w_imag = w[:, : C * C], w[:, C * C :]
    for p in range(X):
        t = totals[p].T
        spec[p] = t
        s_real = widen(t[:K], over_o[...])
        s_imag = widen(t[K:], over_o[...])
        real = narrow(w_real * s_real - w_imag * s_imag, over_i[...])
        imag = narrow(w_real * s_imag + w_imag * s_real, over_i[...])
        put_modes(at, p, modes, real, imag)
    run_gather(at, modes, sems, every)
    for copy in every:
        copy.wait_send()


def unmix_kernel(
    part, w_all, spec, over_o, over_i, small, modes, grad, small_out, b, grad_all, s_small, r_small, small_sems, grad_sem
):
    at = places()
    greet(at)
    sems = (b["sends"], b["recvs"])
    every = []
    small_send, small_recv = small_sems

    groups = [
        [device(at, core=1 - at["core"])],
        [device(at, x=turned(at, "x", s)) for s in (1, 2, 3)],
        [device(at, y=turned(at, "y", s)) for s in (1, 2, 3)],
        [device(at, **to) for to in z_partners(at)],
    ]

    def small_stage(n):
        base = (0, 1, 4, 7)[n]
        return [
            send(s_small.at[n], r_small.at[base + e], (small_send, small_recv), base + e, to)
            for e, to in enumerate(groups[n])
        ]

    def small_sum(n, copies):
        base = (0, 1, 4, 7)[n]
        total = s_small[n]
        for e, copy in enumerate(copies):
            copy.wait_recv()
            total = total + r_small[base + e]
        s_small[n + 1] = total

    s_small[0] = small[...]
    totals = run_scatter(at, part, b, sems, every)
    w = w_all[...].reshape(K, 2 * C * C).astype(F32)
    w_real, w_imag = w[:, : C * C], w[:, C * C :]
    for p in range(X):
        t = totals[p].T * 2.0
        d_real = widen(t[:K], over_i[...])
        d_imag = widen(t[K:], over_i[...])
        real = narrow(w_real * d_real + w_imag * d_imag, over_o[...])
        imag = narrow(w_real * d_imag - w_imag * d_real, over_o[...])
        put_modes(at, p, modes, real * 0.5, imag * 0.5)
        s_real = widen(spec[p, :K], over_o[...])
        s_imag = widen(spec[p, K:], over_o[...])
        g_real = d_real * s_real + d_imag * s_imag
        g_imag = d_imag * s_real - d_real * s_imag
        if p == 0:
            grad_all[:, : C * C] = g_real
            grad_all[:, C * C :] = g_imag
        else:
            grad_all[:, : C * C] += g_real
            grad_all[:, C * C :] += g_imag
    keep = pl.ds(pl.multiple_of(at["hi"] * (K // 2), K // 2), K // 2)
    grad_out = pltpu.make_async_copy(grad_all.at[keep], grad, grad_sem)
    grad_out.start()
    for n in range(4):
        copies = small_stage(n)
        every += copies
        small_sum(n, copies)
    small_out[...] = s_small[4] * (1.0 / math.sqrt(X * Y * Z))
    run_gather(at, modes, sems, every)
    for copy in every:
        copy.wait_send()
    grad_out.wait()


def gelu_terms(v):
    e = jnp.exp(v * v * -0.5)
    t = 1.0 / (1.0 + jnp.abs(v) * (0.3275911 / math.sqrt(2.0)))
    q = t * (0.5 * 1.061405429) - 0.5 * 1.453152027
    q = q * t + 0.5 * 1.421413741
    q = q * t - 0.5 * 0.284496736
    q = q * t + 0.5 * 0.254829592
    q = q * t * e
    phi = jnp.where(v >= 0.0, 1.0 - q, q)
    return v * phi, phi + v * e * (1.0 / math.sqrt(2.0 * math.pi))


def kron_of(weight, over, same):
    wide = dot_nt(dot(over, weight).astype(BF), over)
    return jnp.where(same, wide, 0.0).astype(BF)


def group_masks():
    a = lax.broadcasted_iota(jnp.int32, (C * G, C * G), 0)
    b = lax.broadcasted_iota(jnp.int32, (C * G, C * G), 1)
    same = lax.rem(a, G) == lax.rem(b, G)
    m = lax.broadcasted_iota(jnp.int32, (C * G, C), 0)
    n = lax.broadcasted_iota(jnp.int32, (C * G, C), 1)
    over = (m // G == n).astype(F32).astype(BF)
    return same, over


def middle_kernel(
    field, cot, modes, point, bias, zf, zi, yf, yi,
    out, gp_out, part, small,
    f_buf, c_buf, spread, rows, o_buf, g_buf, wide, kron, bias_col, acc, bias_acc, sems, out_sems,
):
    f_copies = [pltpu.make_async_copy(field.at[:, x], f_buf.at[x], sems.at[0, x]) for x in range(X)]
    c_copies = [pltpu.make_async_copy(cot.at[:, x], c_buf.at[x], sems.at[1, x]) for x in range(X)]
    for x in range(X):
        f_copies[x].start()
        c_copies[x].start()
    same, over = group_masks()
    kron[...] = kron_of(point[...], over, same)
    bias_col[...] = dot(over, bias[...])
    acc[...] = jnp.zeros_like(acc)
    bias_acc[...] = jnp.zeros_like(bias_acc)
    outs = []
    for x in range(X):
        modes_to_rows(modes.at[x], yi, wide, spread)
        f_copies[x].wait()
        c_copies[x].wait()

        @pl.loop(0, NG)
        def _(g):
            at = pl.ds(pl.multiple_of(g * G, G), G)
            f = f_buf[x, :, at, :].reshape(C * G, COLS)
            pre = dot(spread[:, at, :].reshape(C * G, 4 * K), zi[...])
            pre = pre + dot(kron[...], f) + bias_col[:, :1]
            value, slope = gelu_terms(pre)
            o_buf[x, :, at, :] = value.astype(BF).reshape(C, G, COLS)
            gp = (c_buf[x, :, at, :].reshape(C * G, COLS).astype(F32) * slope).astype(BF)
            g_buf[x, :, at, :] = gp.reshape(C, G, COLS)
            wide_gp = gp.astype(F32)
            bias_acc[...] += wide_gp[:, : COLS // 2] + wide_gp[:, COLS // 2 :]
            acc[...] += dot_nt(gp, f)
            rows[:, at, :] = dot(gp, zf[...]).astype(BF).reshape(C, G, 4 * K)

        outs.append(pltpu.make_async_copy(o_buf.at[x], out.at[:, x], out_sems.at[0, x]))
        outs.append(pltpu.make_async_copy(g_buf.at[x], gp_out.at[:, x], out_sems.at[1, x]))
        outs[-2].start()
        outs[-1].start()
        rows_to_modes(lambda c: rows[c], yf, wide, part.at[x])
    kept = jnp.where(same, acc[...], 0.0).reshape(C, G, C * G).sum(axis=1)
    term = jnp.dot(kept, over.astype(F32), precision=lax.Precision.HIGHEST)
    total = bias_acc[...].reshape(C, G, COLS // 2).sum(axis=1).sum(axis=1, keepdims=True)
    small[:, :C] = term
    small[:, C:] = jnp.broadcast_to(total, (C, 2 * K - C))
    for copy in outs:
        copy.wait()


def last_kernel(gp, modes, point_t, zi, yi, out, g_buf, spread, o_buf, wide, kron, sems, out_sems):
    copies = [pltpu.make_async_copy(gp.at[:, x], g_buf.at[x], sems.at[x]) for x in range(X)]
    for copy in copies:
        copy.start()
    same, over = group_masks()
    kron[...] = kron_of(point_t[...], over, same)
    outs = []
    for x in range(X):
        modes_to_rows(modes.at[x], yi, wide, spread)
        copies[x].wait()

        @pl.loop(0, NG)
        def _(g):
            at = pl.ds(pl.multiple_of(g * G, G), G)
            v = dot(spread[:, at, :].reshape(C * G, 4 * K), zi[...])
            v = v + dot(kron[...], g_buf[x, :, at, :].reshape(C * G, COLS))
            o_buf[x, :, at, :] = v.astype(BF).reshape(C, G, COLS)

        outs.append(pltpu.make_async_copy(o_buf.at[x], out.at[:, x], out_sems.at[x]))
        outs[-1].start()
    for copy in outs:
        copy.wait()


VMEM = pl.BlockSpec(memory_space=pltpu.VMEM)
ANY = pl.BlockSpec(memory_space=pl.ANY)
LIMIT = 56 * 1024 * 1024


def params(collective_id=None):
    if collective_id is None:
        return pltpu.CompilerParams(vmem_limit_bytes=LIMIT)
    return pltpu.CompilerParams(
        vmem_limit_bytes=LIMIT, collective_id=collective_id, has_side_effects=True
    )


def grid_buffer(dtype=BF):
    return pltpu.VMEM((X, C, ROWS, COLS), dtype)


def local(field, spec_weight, point_weight, bias, cotangent):
    gy, gz = lax.axis_index("gy"), lax.axis_index("gz")
    zf_all, zi_all, yf_all, yi_all = make_tables()
    zf = lax.dynamic_index_in_dim(jnp.asarray(zf_all), gz, 0, keepdims=False)
    zi = lax.dynamic_index_in_dim(jnp.asarray(zi_all), gz, 0, keepdims=False)
    yf = lax.dynamic_index_in_dim(jnp.asarray(yf_all), gy, 0, keepdims=False)
    yi = lax.dynamic_index_in_dim(jnp.asarray(yi_all), gy, 0, keepdims=False)
    over_o, over_i = (jnp.asarray(t) for t in make_spreads())
    shape = jax.ShapeDtypeStruct
    flat = (X, K, C, 2 * K)
    deep = (X, 2, 4, 4, 2, C, 2 * K)
    wide = pltpu.VMEM((K * C, 2 * K), F32)
    line = pltpu.VMEM((C, ROWS, 4 * K), BF)
    dma = pltpu.SemaphoreType.DMA

    part = pl.pallas_call(
        first_kernel,
        out_shape=shape(flat, BF),
        in_specs=[ANY, VMEM, VMEM],
        out_specs=VMEM,
        scratch_shapes=[grid_buffer(), line, wide, dma((X,))],
        compiler_params=params(),
        name="field_modes",
    )(field, zf, yf)

    modes, spec, w_all = pl.pallas_call(
        mix_kernel,
        out_shape=(shape(deep, BF), shape((X, 2 * K, C), F32), shape((2, K // 2, 2 * C * C), BF)),
        in_specs=[VMEM] * 4,
        out_specs=[VMEM] * 3,
        scratch_shapes=[exchange_scratch(), dma((3,))],
        compiler_params=params(1),
        name="mix_modes",
    )(part.reshape(deep), spec_weight, over_o, over_i)

    bias_in = jnp.broadcast_to(bias[:, None], (C, 2 * K))
    output, grad_pre, part2, small = pl.pallas_call(
        middle_kernel,
        out_shape=(
            shape(field.shape, BF),
            shape(field.shape, BF),
            shape(flat, BF),
            shape((C, 2 * K), F32),
        ),
        in_specs=[ANY, ANY] + [VMEM] * 7,
        out_specs=[ANY, ANY, VMEM, VMEM],
        scratch_shapes=[
            grid_buffer(), grid_buffer(), line, line, grid_buffer(), grid_buffer(), wide,
            pltpu.VMEM((C * G, C * G), BF),
            pltpu.VMEM((C * G, 2 * K), F32),
            pltpu.VMEM((C * G, C * G), F32),
            pltpu.VMEM((C * G, COLS // 2), F32),
            dma((2, X)),
            dma((2, X)),
        ],
        compiler_params=params(),
        name="layer",
    )(field, cotangent, modes.reshape(flat), point_weight, bias_in, zf, zi, yf, yi)

    modes2, grad_spec, small_out = pl.pallas_call(
        unmix_kernel,
        out_shape=(
            shape(deep, BF),
            shape((K // 2, 2 * C * C), F32),
            shape((C, 2 * K), F32),
        ),
        in_specs=[VMEM] * 6,
        out_specs=[VMEM, ANY, VMEM],
        scratch_shapes=[
            exchange_scratch(),
            pltpu.VMEM((K, 2 * C * C), F32),
            pltpu.VMEM((5, C, 2 * K), F32),
            pltpu.VMEM((10, C, 2 * K), F32),
            [dma((10,)), dma((10,))],
            dma,
        ],
        compiler_params=params(2),
        name="unmix_modes",
    )(part2.reshape(deep), w_all, spec, over_o, over_i, small)

    grad_input = pl.pallas_call(
        last_kernel,
        out_shape=shape(field.shape, BF),
        in_specs=[ANY] + [VMEM] * 4,
        out_specs=ANY,
        scratch_shapes=[
            grid_buffer(), line, grid_buffer(), wide,
            pltpu.VMEM((C * G, C * G), BF),
            dma((X,)),
            dma((X,)),
        ],
        compiler_params=params(),
        name="input_gradient",
    )(grad_pre, modes2.reshape(flat), point_weight.T, zi, yi)

    return output, grad_input, grad_spec, small_out[:, :C], small_out[:, C]


def solution(mesh):
    grid = P(None, None, "gy", "gz")
    owned = P(("gy", "gz"), None)
    return jax.shard_map(
        local,
        mesh=mesh,
        in_specs=(grid, owned, P(), P(), grid),
        out_specs=(grid, grid, owned, P(), P()),
        check_vma=False,
    )
```

```python
import functools
import math

import jax
import jax.numpy as jnp
import numpy as np
from jax import lax
from jax.experimental import pallas as pl
from jax.experimental.pallas import tpu as pltpu

P = jax.sharding.PartitionSpec
BF = jnp.bfloat16
F32 = jnp.float32

C = 32
X = 2
Y = 2048
Z = 2048
K = 64
ROWS = 128
COLS = 256
G = 16
NG = ROWS // G

MESH = pl.DeviceIdType.MESH


def row_order():
    order = []
    for core in range(2):
        for cx in range(4):
            for cy in range(4):
                for lo in range(2):
                    order.append(cx * 16 + lo * 8 + core * 4 + cy)
    return np.array(order)


def make_tables():
    j = row_order()
    fy = np.where(j < K // 2, j, Y - K + j)
    y = np.arange(Y)
    ang_y = 2.0 * np.pi * ((fy[:, None] * y[None, :]) % Y) / Y
    z = np.arange(Z)
    ang_z = 2.0 * np.pi * ((np.arange(K)[:, None] * z[None, :]) % Z) / Z
    cy, sy = np.cos(ang_y), np.sin(ang_y)
    cz, sz = np.cos(ang_z), np.sin(ang_z)
    zf = np.concatenate([cz, -sz, -sz, -cz], axis=0)
    zf = zf.reshape(4 * K, Z // COLS, COLS).transpose(1, 0, 2)
    yf = np.stack([cy, sy], axis=0).reshape(2, K, Y // ROWS, ROWS)
    yf = yf.transpose(2, 1, 0, 3).reshape(Y // ROWS, K, 2 * ROWS)
    yi = np.stack([cy, sy], axis=0).reshape(2, K, Y // ROWS, ROWS)
    yi = yi.transpose(2, 0, 3, 1).reshape(Y // ROWS, 2 * ROWS, K)
    bf = lambda a: np.ascontiguousarray(a).astype(jnp.bfloat16)
    scale = 1.0 / math.sqrt(Y * Z)
    return (
        bf(zf.transpose(0, 2, 1)),
        bf(zf),
        bf(yf * scale),
        bf(yi * (2.0 * scale)),
    )


def make_spreads():
    lane = np.arange(C * C)
    rows = np.arange(C)[:, None]
    over_o = (lane[None, :] // C == rows).astype(np.float32)
    over_i = (lane[None, :] % C == rows).astype(np.float32)
    return over_o.astype(jnp.bfloat16), over_i.astype(jnp.bfloat16)


def dot(a, b):
    return jnp.dot(a, b, preferred_element_type=F32)


def dot_nt(a, b):
    return lax.dot_general(a, b, (((1,), (1,)), ((), ())), preferred_element_type=F32)


def split(v):
    hi = v.astype(BF)
    return hi, (v - hi.astype(F32)).astype(BF)


def forward_z(src, zf, rows):
    for c in range(0, C, 4):
        f = src[pl.ds(c, 4)].reshape(4 * ROWS, COLS)
        rows[pl.ds(c, 4)] = dot(f, zf[...]).astype(BF).reshape(4, ROWS, 4 * K)


def forward_y(rows, yf, wide, part):
    for c in range(0, C, 2):
        one, two = rows[c], rows[c + 1]
        upper = jnp.concatenate([one[:, : 2 * K], two[:, : 2 * K]], axis=1)
        lower = jnp.concatenate([one[:, 2 * K :], two[:, 2 * K :]], axis=1)
        r = dot(yf[...], jnp.concatenate([upper, lower], axis=0))
        wide[pl.ds(c, K, stride=C), :] = r[:, : 2 * K]
        wide[pl.ds(c + 1, K, stride=C), :] = r[:, 2 * K :]
    step = K * C // 8
    for n in range(8):
        part[n // 4, n % 4] = wide[pl.ds(n * step, step), :].astype(BF).reshape(4, 2, C, 2 * K)


def inverse_y(modes, yi, wide, spread):
    step = K * C // 8
    for n in range(8):
        wide[pl.ds(n * step, step), :] = modes[n // 4, n % 4].astype(F32).reshape(step, 2 * K)
    for c in range(0, C, 2):
        one = wide[pl.ds(c, K, stride=C), :].astype(BF)
        two = wide[pl.ds(c + 1, K, stride=C), :].astype(BF)
        r = dot(yi[...], jnp.concatenate([one, two], axis=1)).astype(BF)
        for e in range(2):
            lanes = slice(e * 2 * K, (e + 1) * 2 * K)
            spread[c + e, :, : 2 * K] = r[:ROWS, lanes]
            spread[c + e, :, 2 * K :] = r[ROWS:, lanes]


def rows_of(g):
    return pl.ds(g * G, G)


def places():
    gy, gz = lax.axis_index("gy"), lax.axis_index("gz")
    return dict(x=gy // 4, lo=gy // 2 % 2, core=gy % 2, y=gz // 2, hi=gz % 2)


def device(at, **other):
    at = dict(at, **other)
    return {
        "gy": at["x"] * 4 + at["lo"] * 2 + at["core"],
        "gz": at["y"] * 2 + at["hi"],
    }


def turned(at, axis, step):
    return lax.rem(at[axis] + step, 4)


STEPS = [(dx, dy, dl) for dx in (2, 1, 3, 0) for dy in (2, 1, 3, 0) for dl in (1, 0)][:-1]


def moved(at, step):
    dx, dy, dl = step
    lo = 1 - at["lo"] if dl else at["lo"]
    return dict(x=turned(at, "x", dx), y=turned(at, "y", dy), lo=lo)


def greet(at):
    barrier = pltpu.get_barrier_semaphore()
    partners = [device(at, core=1 - at["core"]), device(at, hi=1 - at["hi"])]
    partners += [device(at, **moved(at, step)) for step in STEPS]
    for partner in partners:
        pl.semaphore_signal(barrier, inc=1, device_id=partner, device_id_type=MESH)
    return barrier, len(partners)


def send(src, dst, sems, n, to):
    send_sem, recv_sem = sems
    copy = pltpu.make_async_remote_copy(
        src_ref=src,
        dst_ref=dst,
        send_sem=send_sem.at[n],
        recv_sem=recv_sem.at[n],
        device_id=to,
        device_id_type=MESH,
    )
    copy.start()
    return copy


def arrived(copies):
    for copy in copies:
        copy.wait()


def scatter_core(at, p, part, b):
    other = 1 - at["core"]
    return [send(part.at[p, other], b["r1"].at[p], b["core_in"], p, device(at, core=other))]


def scatter_rows(at, p, part, b):
    me = at["core"]
    for cx in range(4):
        b["s1"][p, cx] = (part[p, me, cx].astype(F32) + b["r1"][p, cx].astype(F32)).astype(BF)
    copies = []
    for n, step in enumerate(STEPS):
        to = moved(at, step)
        copies.append(
            send(
                b["s1"].at[p, to["x"], to["y"], to["lo"]],
                b["r2"].at[p, n],
                b["rows_in"],
                p * len(STEPS) + n,
                device(at, **to),
            )
        )
    return copies


def scatter_halves(at, p, b):
    total = b["s1"][p, at["x"], at["y"], at["lo"]].astype(F32)
    for n in range(len(STEPS)):
        total = total + b["r2"][p, n].astype(F32)
    b["s3"][p] = total
    return [send(b["s3"].at[p], b["r4"].at[p], b["half_in"], p, device(at, hi=1 - at["hi"]))]


def scatter_total(at, p, b):
    return b["s3"][p] + b["r4"][p]


def gather_rows(at, p, modes, b):
    here = modes.at[p, at["core"], at["x"], at["y"], at["lo"]]
    return [
        send(here, here, b["rows_out"], p * len(STEPS) + n, device(at, **moved(at, step)))
        for n, step in enumerate(STEPS)
    ]


def gather_core(at, p, modes, b, copies):
    passed = []
    for dx in (0, 1, 3, 2):
        arrived([copy for copy, step in zip(copies, STEPS) if step[0] == dx])
        block = modes.at[p, at["core"], turned(at, "x", 4 - dx)]
        passed.append(send(block, block, b["core_out"], 4 * p + dx, device(at, core=1 - at["core"])))
    return passed


def exchange_scratch():
    pair = lambda n: [pltpu.SemaphoreType.DMA((n,)), pltpu.SemaphoreType.DMA((n,))]
    rows = len(STEPS)
    return dict(
        r1=pltpu.VMEM((X, 4, 4, 2, C, 2 * K), BF),
        s1=pltpu.VMEM((X, 4, 4, 2, C, 2 * K), BF),
        r2=pltpu.VMEM((X, rows, C, 2 * K), BF),
        s3=pltpu.VMEM((X, C, 2 * K), F32),
        r4=pltpu.VMEM((X, C, 2 * K), F32),
        core_in=pair(X),
        rows_in=pair(X * rows),
        half_in=pair(X),
        rows_out=pair(X * rows),
        core_out=pair(4 * X),
    )


def widen(v, table):
    hi, lo = split(v)
    return dot(hi, table) + dot(lo, table)


def narrow(v, table):
    hi, lo = split(v)
    return dot_nt(hi, table) + dot_nt(lo, table)


def put_modes(at, p, modes, real, imag):
    block = jnp.concatenate([real, imag], axis=0).T
    modes[p, at["core"], at["x"], at["y"], at["lo"]] = block.astype(BF)


def mix(at, p, total, w_all, over_o, over_i, modes, spec):
    t = total.T
    spec[p] = t
    s_real = widen(t[:K], over_o)
    s_imag = widen(t[K:], over_o)
    w_real, w_imag = w_all[:, : C * C].astype(F32), w_all[:, C * C :].astype(F32)
    real = narrow(w_real * s_real - w_imag * s_imag, over_i)
    imag = narrow(w_real * s_imag + w_imag * s_real, over_i)
    put_modes(at, p, modes, real, imag)


def unmix(at, p, total, w_all, over_o, over_i, modes, dual):
    t = total.T * 2.0
    dual[p] = t
    d_real = widen(t[:K], over_i)
    d_imag = widen(t[K:], over_i)
    w_real, w_imag = w_all[:, : C * C].astype(F32), w_all[:, C * C :].astype(F32)
    real = narrow(w_real * d_real + w_imag * d_imag, over_o)
    imag = narrow(w_real * d_imag - w_imag * d_real, over_o)
    put_modes(at, p, modes, real * 0.5, imag * 0.5)


def weight_gradient(at, spec, dual, over_o, over_i, grad):
    half = K // 2
    real, imag = 0.0, 0.0
    for p in range(X):
        top = pl.ds(pl.multiple_of(at["hi"] * half, half), half)
        low = pl.ds(pl.multiple_of(at["hi"] * half + K, half), half)
        s_real, s_imag = widen(spec[p, top], over_o), widen(spec[p, low], over_o)
        d_real, d_imag = widen(dual[p, top], over_i), widen(dual[p, low], over_i)
        real = real + d_real * s_real + d_imag * s_imag
        imag = imag + d_imag * s_real - d_real * s_imag
    grad[:, : C * C] = real
    grad[:, C * C :] = imag


def gelu_terms(v):
    e = jnp.exp(v * v * -0.5)
    t = 1.0 / (1.0 + jnp.abs(v) * (0.3275911 / math.sqrt(2.0)))
    q = t * (0.5 * 1.061405429) - 0.5 * 1.453152027
    q = q * t + 0.5 * 1.421413741
    q = q * t - 0.5 * 0.284496736
    q = q * t + 0.5 * 0.254829592
    q = q * t * e
    phi = jnp.where(v >= 0.0, 1.0 - q, q)
    return v * phi, phi + v * e * (1.0 / math.sqrt(2.0 * math.pi))


def group_masks():
    a = lax.broadcasted_iota(jnp.int32, (C * G, C * G), 0)
    b = lax.broadcasted_iota(jnp.int32, (C * G, C * G), 1)
    same = lax.rem(a, G) == lax.rem(b, G)
    m = lax.broadcasted_iota(jnp.int32, (C * G, C), 0)
    n = lax.broadcasted_iota(jnp.int32, (C * G, C), 1)
    over = (m // G == n).astype(F32).astype(BF)
    return same, over


def kron_of(half, over, same):
    return jnp.where(same, dot_nt(half.astype(BF), over), 0.0).astype(BF)


def pointwise(f_buf, kron, bias_col, base):
    for g in range(NG):
        f = f_buf[:, rows_of(g), :].reshape(C * G, COLS)
        base[g] = dot(kron[...], f) + bias_col[:, :1]


def layer(spread, base, cot, zi, zf, o_buf, g_buf, rows, between=None):
    pre, slope_of = {}, {}
    for s in range(NG + 2):
        if s < NG:
            pre[s] = dot(spread[:, rows_of(s), :].reshape(C * G, 4 * K), zi[...]) + base[s]
        if 1 <= s <= NG:
            at = rows_of(s - 1)
            value, slope = gelu_terms(pre.pop(s - 1))
            o_buf[:, at, :] = value.astype(BF).reshape(C, G, COLS)
            gp = (cot[:, at, :].reshape(C * G, COLS).astype(F32) * slope).astype(BF)
            g_buf[:, at, :] = gp.reshape(C, G, COLS)
            slope_of[s - 1] = gp
        if s >= 2:
            r = dot(slope_of.pop(s - 2), zf[...]).astype(BF)
            rows[:, rows_of(s - 2), :] = r.reshape(C, G, 4 * K)
        if between is not None and s == NG // 2:
            between()


def point_gradient(g_buf, f_buf, acc, bias_acc, first):
    total, sums = 0.0, 0.0
    for q in range(0, NG, 4):
        gs = [g_buf[:, rows_of(q + e), :].reshape(C * G, COLS) for e in range(4)]
        fs = [f_buf[:, rows_of(q + e), :].reshape(C * G, COLS) for e in range(4)]
        total = total + dot_nt(jnp.concatenate(gs, axis=1), jnp.concatenate(fs, axis=1))
        for gp in gs:
            gp = gp.astype(F32)
            sums = sums + gp[:, : COLS // 2] + gp[:, COLS // 2 :]
    acc[...] = total if first else acc[...] + total
    bias_acc[...] = sums if first else bias_acc[...] + sums


def main_kernel(
    field, cot, weights, zf_all, zi_all, yf_all, yi_all, point, bias, over_o_ref, over_i_ref,
    out, gp_out, modes_out, grad, small_out,
    f_buf, c_buf, spread, rows, o_buf, g_buf, base, wide, part, modes, part2, modes2,
    zf, zi, yf, yi, kron, bias_col, acc, bias_acc, w_all, spec, dual, grad_buf, s_small, r_small,
    b1, b2, sems, w_sems, small_sems, out_sems,
):
    at = places()
    gy, gz = lax.axis_index("gy"), lax.axis_index("gz")
    local = pltpu.make_async_copy
    loads = [
        local(field.at[:, 0], f_buf.at[0], sems.at[0]),
        local(zf_all.at[gz], zf, sems.at[1]),
        local(yf_all.at[gy], yf, sems.at[2]),
        local(field.at[:, 1], f_buf.at[1], sems.at[3]),
        local(weights, w_all.at[at["hi"]], sems.at[4]),
        local(zi_all.at[gz], zi, sems.at[5]),
        local(yi_all.at[gy], yi, sems.at[6]),
        local(cot.at[:, 0], c_buf.at[0], sems.at[7]),
        local(cot.at[:, 1], c_buf.at[1], sems.at[8]),
    ]
    for load in loads[:4]:
        load.start()
    barrier, partners = greet(at)
    same, over = group_masks()
    kron[...] = kron_of(dot(over, point[...]), over, same)
    bias_wide = jnp.broadcast_to(bias[...].astype(F32), (2 * K, C)).astype(BF)
    bias_col[...] = dot_nt(over, bias_wide)
    over_o, over_i = over_o_ref[...], over_i_ref[...]

    for n in range(3):
        loads[n].wait()
    forward_z(f_buf.at[0], zf, rows.at[0])
    forward_y(rows.at[0], yf, wide.at[0], part.at[0])
    pl.semaphore_wait(barrier, partners)
    f0 = scatter_core(at, 0, part, b1)
    loads[3].wait()
    for load in loads[4:]:
        load.start()
    w_there = pltpu.make_async_remote_copy(
        src_ref=weights,
        dst_ref=w_all.at[at["hi"]],
        send_sem=w_sems.at[0],
        recv_sem=w_sems.at[1],
        device_id=device(at, hi=1 - at["hi"]),
        device_id_type=MESH,
    )
    forward_z(f_buf.at[1], zf, rows.at[1])
    arrived(f0)
    f0 = scatter_rows(at, 0, part, b1)
    forward_y(rows.at[1], yf, wide.at[1], part.at[1])
    f1 = scatter_core(at, 1, part, b1)
    w_there.start()
    pointwise(f_buf.at[0], kron, bias_col, base.at[0])
    arrived(f1)
    f1 = scatter_rows(at, 1, part, b1)
    pointwise(f_buf.at[1], kron, bias_col, base.at[1])
    arrived(f0)
    f0 = scatter_halves(at, 0, b1)
    arrived(f1)
    f1 = scatter_halves(at, 1, b1)
    for load in loads[4:]:
        load.wait()
    w_there.wait()
    w = w_all[...].reshape(K, 2 * C * C)
    arrived(f0)
    mix(at, 0, scatter_total(at, 0, b1), w, over_o, over_i, modes, spec)
    f0 = gather_rows(at, 0, modes, b1)
    arrived(f1)
    mix(at, 1, scatter_total(at, 1, b1), w, over_o, over_i, modes, spec)
    f1 = gather_rows(at, 1, modes, b1)
    f0 = gather_core(at, 0, modes, b1, f0)

    arrived(f0)
    inverse_y(modes.at[0], yi, wide.at[0], spread.at[0])
    f1 = gather_core(at, 1, modes, b1, f1)
    layer(spread.at[0], base.at[0], c_buf.at[0], zi, zf, o_buf.at[0], g_buf.at[0], rows.at[0])
    forward_y(rows.at[0], yf, wide.at[0], part2.at[0])
    f0 = scatter_core(at, 0, part2, b2)
    outs = [
        local(o_buf.at[0], out.at[:, 0], out_sems.at[0]),
        local(g_buf.at[0], gp_out.at[:, 0], out_sems.at[1]),
    ]
    outs[0].start()
    outs[1].start()
    arrived(f1)
    inverse_y(modes.at[1], yi, wide.at[1], spread.at[1])
    arrived(f0)
    f0 = scatter_rows(at, 0, part2, b2)
    layer(spread.at[1], base.at[1], c_buf.at[1], zi, zf, o_buf.at[1], g_buf.at[1], rows.at[1])
    forward_y(rows.at[1], yf, wide.at[1], part2.at[1])
    f1 = scatter_core(at, 1, part2, b2)
    outs += [
        local(o_buf.at[1], out.at[:, 1], out_sems.at[2]),
        local(g_buf.at[1], gp_out.at[:, 1], out_sems.at[3]),
    ]
    outs[2].start()
    outs[3].start()
    arrived(f0)
    f0 = scatter_halves(at, 0, b2)

    groups = [
        [device(at, core=1 - at["core"])],
        [device(at, x=turned(at, "x", s)) for s in (1, 2, 3)],
        [device(at, y=turned(at, "y", s)) for s in (1, 2, 3)],
        [device(at, lo=1 - at["lo"])],
        [device(at, hi=1 - at["hi"])],
    ]
    bases = (0, 1, 4, 7, 8)

    def small_send(n):
        return [
            send(s_small.at[n], r_small.at[bases[n] + e], small_sems, bases[n] + e, to)
            for e, to in enumerate(groups[n])
        ]

    def small_sum(n, copies):
        arrived(copies)
        total = s_small[n]
        for e in range(len(copies)):
            total = total + r_small[bases[n] + e]
        s_small[n + 1] = total

    arrived(f1)
    f1 = scatter_rows(at, 1, part2, b2)
    point_gradient(g_buf.at[0], f_buf.at[0], acc, bias_acc, True)
    arrived(f0)
    unmix(at, 0, scatter_total(at, 0, b2), w, over_o, over_i, modes2, dual)
    f0 = gather_rows(at, 0, modes2, b2)
    point_gradient(g_buf.at[1], f_buf.at[1], acc, bias_acc, False)
    arrived(f1)
    f1 = scatter_halves(at, 1, b2)
    kept = jnp.where(same, acc[...], 0.0).reshape(C, G, C * G).sum(axis=1)
    term = jnp.dot(kept, over.astype(F32), precision=lax.Precision.HIGHEST)
    total = bias_acc[...].reshape(C, G, COLS // 2).sum(axis=1).sum(axis=1, keepdims=True)
    s_small[0, :, :C] = term
    s_small[0, :, C:] = jnp.broadcast_to(total, (C, 2 * K - C))
    small = small_send(0)
    arrived(f1)
    unmix(at, 1, scatter_total(at, 1, b2), w, over_o, over_i, modes2, dual)
    f1 = gather_rows(at, 1, modes2, b2)
    small_sum(0, small)
    small = small_send(1)
    f0 = gather_core(at, 0, modes2, b2, f0)
    weight_gradient(at, spec, dual, over_o, over_i, grad_buf)
    outs.append(local(grad_buf, grad, out_sems.at[4]))
    outs[-1].start()
    small_sum(1, small)
    small = small_send(2)
    arrived(f0)
    outs.append(local(modes2.at[0], modes_out.at[0], out_sems.at[5]))
    outs[-1].start()
    small_sum(2, small)
    small = small_send(3)
    f1 = gather_core(at, 1, modes2, b2, f1)
    small_sum(3, small)
    small = small_send(4)
    arrived(f1)
    outs.append(local(modes2.at[1], modes_out.at[1], out_sems.at[6]))
    outs[-1].start()
    small_sum(4, small)
    small_out[...] = s_small[5] * (1.0 / math.sqrt(X * Y * Z))
    for copy in outs:
        copy.wait()


def last_kernel(
    held, gp, modes_in, zi_all, yi_all, grad_in, point, small,
    out, output, grad, term, total, modes, g_buf, h_buf, w_buf, spread, o_buf, wide, zi, yi, kron, sems, out_sems,
):
    gy, gz = lax.axis_index("gy"), lax.axis_index("gz")
    local = pltpu.make_async_copy
    loads = [
        local(modes_in.at[0], modes.at[0], sems.at[0]),
        local(yi_all.at[gy], yi, sems.at[1]),
        local(zi_all.at[gz], zi, sems.at[2]),
        local(gp.at[:, 0], g_buf.at[0], sems.at[3]),
        local(modes_in.at[1], modes.at[1], sems.at[4]),
        local(gp.at[:, 1], g_buf.at[1], sems.at[5]),
    ]
    passing = [local(held.at[:, x], h_buf.at[x], sems.at[6 + x]) for x in range(X)]
    passing.append(local(grad_in, w_buf, sems.at[8]))
    for load in loads + passing:
        load.start()
    term[...] = small[:, :C]
    total[...] = small[...].T[C : C + 1]
    same, over = group_masks()
    kron[...] = kron_of(dot_nt(over, point[...]), over, same)
    outs = []
    for x in range(X):
        for load in loads[:4] if x == 0 else loads[4:]:
            load.wait()
        inverse_y(modes.at[x], yi, wide.at[x], spread.at[x])
        for g in range(NG):
            at = rows_of(g)
            v = dot(spread[x, :, at, :].reshape(C * G, 4 * K), zi[...])
            v = v + dot(kron[...], g_buf[x, :, at, :].reshape(C * G, COLS))
            o_buf[x, :, at, :] = v.astype(BF).reshape(C, G, COLS)
        passing[x].wait()
        outs.append(local(h_buf.at[x], output.at[:, x], out_sems.at[2 + x]))
        outs[-1].start()
        outs.append(local(o_buf.at[x], out.at[:, x], out_sems.at[x]))
        outs[-1].start()
    passing[2].wait()
    outs.append(local(w_buf, grad, out_sems.at[4]))
    outs[-1].start()
    for copy in outs:
        copy.wait()


VMEM = pl.BlockSpec(memory_space=pltpu.VMEM)
ANY = pl.BlockSpec(memory_space=pl.ANY)
LIMIT = 60 * 1024 * 1024


def params(collective_id=None):
    if collective_id is None:
        return pltpu.CompilerParams(vmem_limit_bytes=LIMIT)
    return pltpu.CompilerParams(
        vmem_limit_bytes=LIMIT, collective_id=collective_id, has_side_effects=True
    )


def grid_buffer(dtype=BF):
    return pltpu.VMEM((X, C, ROWS, COLS), dtype)


def local(field, spec_weight, point_weight, bias, cotangent):
    zf, zi, yf, yi = (jnp.asarray(t) for t in make_tables())
    over_o, over_i = (jnp.asarray(t) for t in make_spreads())
    shape = jax.ShapeDtypeStruct
    deep = (X, 2, 4, 4, 2, C, 2 * K)
    lines = pltpu.VMEM((X, C, ROWS, 4 * K), BF)
    wide = pltpu.VMEM((X, K * C, 2 * K), F32)
    table = pltpu.VMEM((COLS, COLS), BF)
    vmem = pltpu.VMEM
    dma = pltpu.SemaphoreType.DMA
    square = (C * G, C * G)

    held, grad_pre, modes, grad_spec, small = pl.pallas_call(
        main_kernel,
        out_shape=(
            shape(field.shape, BF),
            shape(field.shape, BF),
            shape(deep, BF),
            shape((K // 2, 2 * C * C), F32),
            shape((C, 2 * K), F32),
        ),
        in_specs=[ANY] * 7 + [VMEM] * 4,
        out_specs=[ANY] * 4 + [VMEM],
        scratch_shapes=[
            grid_buffer(), grid_buffer(), lines, lines, grid_buffer(), grid_buffer(),
            vmem((X, NG, C * G, COLS), F32),
            wide, vmem(deep, BF), vmem(deep, BF), vmem(deep, BF), vmem(deep, BF),
            table, table, vmem((K, 2 * ROWS), BF), vmem((2 * ROWS, K), BF),
            vmem(square, BF), vmem((C * G, 2 * K), F32), vmem(square, F32),
            vmem((C * G, COLS // 2), F32),
            vmem((2, K // 2, 2 * C * C), BF),
            vmem((X, 2 * K, C), F32), vmem((X, 2 * K, C), F32),
            vmem((K // 2, 2 * C * C), F32),
            vmem((6, C, 2 * K), F32), vmem((9, C, 2 * K), F32),
            exchange_scratch(), exchange_scratch(),
            dma((9,)), dma((2,)), [dma((9,)), dma((9,))], dma((7,)),
        ],
        compiler_params=params(1),
        name="layer",
    )(
        field, cotangent, spec_weight, zf, zi, yf, yi,
        point_weight, bias.reshape(1, C), over_o, over_i,
    )

    grad_input, output, grad, term, total = pl.pallas_call(
        last_kernel,
        out_shape=(
            shape(field.shape, BF),
            shape(field.shape, BF),
            shape(grad_spec.shape, F32),
            shape((C, C), F32),
            shape((1, C), F32),
        ),
        in_specs=[ANY] * 6 + [VMEM] * 2,
        out_specs=[ANY] * 3 + [VMEM] * 2,
        scratch_shapes=[
            vmem(deep, BF), grid_buffer(), grid_buffer(), vmem(grad_spec.shape, F32),
            lines, grid_buffer(), wide,
            table, vmem((2 * ROWS, K), BF), vmem(square, BF), dma((9,)), dma((5,)),
        ],
        compiler_params=params(),
        name="input_gradient",
    )(held, grad_pre, modes, zi, yi, grad_spec, point_weight, small)

    return output, grad_input, grad, term, total.reshape(C)


def solution(mesh):
    grid = P(None, None, "gy", "gz")
    owned = P(("gy", "gz"), None)
    return jax.shard_map(
        local,
        mesh=mesh,
        in_specs=(grid, owned, P(), P(), grid),
        out_specs=(grid, grid, owned, P(), P()),
        check_vma=False,
    )
```

```python
import functools
import math

import jax
import jax.numpy as jnp
import numpy as np
from jax import lax
from jax.experimental import pallas as pl
from jax.experimental.pallas import tpu as pltpu

P = jax.sharding.PartitionSpec
BF = jnp.bfloat16
F32 = jnp.float32

C = 32
X = 2
Y = 2048
Z = 2048
K = 64
ROWS = 128
COLS = 256
G = 16
NG = ROWS // G

MESH = pl.DeviceIdType.MESH


def row_order():
    order = []
    for core in range(2):
        for cx in range(4):
            for cy in range(4):
                for lo in range(2):
                    order.append(cx * 16 + lo * 8 + core * 4 + cy)
    return np.array(order)


def make_tables():
    j = row_order()
    fy = np.where(j < K // 2, j, Y - K + j)
    y = np.arange(Y)
    ang_y = 2.0 * np.pi * ((fy[:, None] * y[None, :]) % Y) / Y
    z = np.arange(Z)
    ang_z = 2.0 * np.pi * ((np.arange(K)[:, None] * z[None, :]) % Z) / Z
    cy, sy = np.cos(ang_y), np.sin(ang_y)
    cz, sz = np.cos(ang_z), np.sin(ang_z)
    zf = np.concatenate([cz, -sz, -sz, -cz], axis=0)
    zf = zf.reshape(4 * K, Z // COLS, COLS).transpose(1, 0, 2)
    yf = np.stack([cy, sy], axis=0).reshape(2, K, Y // ROWS, ROWS)
    yf = yf.transpose(2, 1, 0, 3).reshape(Y // ROWS, K, 2 * ROWS)
    yi = np.stack([cy, sy], axis=0).reshape(2, K, Y // ROWS, ROWS)
    yi = yi.transpose(2, 0, 3, 1).reshape(Y // ROWS, 2 * ROWS, K)
    bf = lambda a: np.ascontiguousarray(a).astype(jnp.bfloat16)
    scale = 1.0 / math.sqrt(Y * Z)
    return (
        bf(zf.transpose(0, 2, 1)),
        bf(zf),
        bf(yf * scale),
        bf(yi * (2.0 * scale)),
    )


def make_spreads():
    lane = np.arange(C * C)
    rows = np.arange(C)[:, None]
    over_o = (lane[None, :] // C == rows).astype(np.float32)
    over_i = (lane[None, :] % C == rows).astype(np.float32)
    return over_o.astype(jnp.bfloat16), over_i.astype(jnp.bfloat16)


def dot(a, b):
    return jnp.dot(a, b, preferred_element_type=F32)


def dot_nt(a, b):
    return lax.dot_general(a, b, (((1,), (1,)), ((), ())), preferred_element_type=F32)


def split(v):
    hi = v.astype(BF)
    return hi, (v - hi.astype(F32)).astype(BF)


def forward_z(src, zf, rows, begin, end):
    for c in range(begin, end, 4):
        f = src[pl.ds(c, 4)].reshape(4 * ROWS, COLS)
        rows[pl.ds(c, 4)] = dot(f, zf[...]).astype(BF).reshape(4, ROWS, 4 * K)


def forward_y(rows, yf, wide, part):
    for c in range(0, C, 2):
        one, two = rows[c], rows[c + 1]
        upper = jnp.concatenate([one[:, : 2 * K], two[:, : 2 * K]], axis=1)
        lower = jnp.concatenate([one[:, 2 * K :], two[:, 2 * K :]], axis=1)
        r = dot(yf[...], jnp.concatenate([upper, lower], axis=0))
        wide[pl.ds(c, K, stride=C), :] = r[:, : 2 * K]
        wide[pl.ds(c + 1, K, stride=C), :] = r[:, 2 * K :]
    step = K * C // 8
    for n in range(8):
        part[n // 4, n % 4] = wide[pl.ds(n * step, step), :].astype(BF).reshape(4, 2, C, 2 * K)


def inverse_y(modes, yi, wide, spread):
    step = K * C // 8
    for n in range(8):
        wide[pl.ds(n * step, step), :] = modes[n // 4, n % 4].astype(F32).reshape(step, 2 * K)
    for c in range(0, C, 2):
        one = wide[pl.ds(c, K, stride=C), :].astype(BF)
        two = wide[pl.ds(c + 1, K, stride=C), :].astype(BF)
        r = dot(yi[...], jnp.concatenate([one, two], axis=1)).astype(BF)
        for e in range(2):
            lanes = slice(e * 2 * K, (e + 1) * 2 * K)
            spread[c + e, :, : 2 * K] = r[:ROWS, lanes]
            spread[c + e, :, 2 * K :] = r[ROWS:, lanes]


def fold(v):
    return jnp.concatenate([v[8 * n : 8 * n + 8] for n in range(C // 8)], axis=1)


def unfold(v):
    return jnp.concatenate([v[:, C * n : C * n + C] for n in range(C // 8)], axis=0)


def rows_of(g):
    return pl.ds(g * G, G)


def places():
    gy, gz = lax.axis_index("gy"), lax.axis_index("gz")
    return dict(x=gy // 4, lo=gy // 2 % 2, core=gy % 2, y=gz // 2, hi=gz % 2)


def device(at, **other):
    at = dict(at, **other)
    return {
        "gy": at["x"] * 4 + at["lo"] * 2 + at["core"],
        "gz": at["y"] * 2 + at["hi"],
    }


def turned(at, axis, step):
    return lax.rem(at[axis] + step, 4)


STEPS = [(dx, dy, dl) for dx in (2, 1, 3, 0) for dy in (2, 1, 3, 0) for dl in (1, 0)][:-1]


def moved(at, step):
    dx, dy, dl = step
    lo = 1 - at["lo"] if dl else at["lo"]
    return dict(x=turned(at, "x", dx), y=turned(at, "y", dy), lo=lo)


def across(at):
    core, hi = 1 - at["core"], 1 - at["hi"]
    return [device(at, core=core), device(at, hi=hi), device(at, core=core, hi=hi)]


def greet(at):
    barrier = pltpu.get_barrier_semaphore()
    partners = across(at) + [device(at, **moved(at, step)) for step in STEPS]
    for partner in partners:
        pl.semaphore_signal(barrier, inc=1, device_id=partner, device_id_type=MESH)
    return barrier, len(partners)


def send(src, dst, sems, n, to):
    send_sem, recv_sem = sems
    copy = pltpu.make_async_remote_copy(
        src_ref=src,
        dst_ref=dst,
        send_sem=send_sem.at[n],
        recv_sem=recv_sem.at[n],
        device_id=to,
        device_id_type=MESH,
    )
    copy.start()
    return copy


def arrived(copies):
    for copy in copies:
        copy.wait()


def scatter_core(at, p, part, b):
    other = 1 - at["core"]
    return [send(part.at[p, other], b["r1"].at[p], b["core_in"], p, device(at, core=other))]


def scatter_rows(at, p, part, b):
    me = at["core"]
    for cx in range(4):
        b["s1"][p, cx] = (part[p, me, cx].astype(F32) + b["r1"][p, cx].astype(F32)).astype(BF)
    copies = []
    for n, step in enumerate(STEPS):
        to = moved(at, step)
        copies.append(
            send(
                b["s1"].at[p, to["x"], to["y"], to["lo"]],
                b["r2"].at[p, n],
                b["rows_in"],
                p * len(STEPS) + n,
                device(at, **to),
            )
        )
    return copies


def scatter_halves(at, p, b):
    total = b["s1"][p, at["x"], at["y"], at["lo"]].astype(F32)
    for n in range(len(STEPS)):
        total = total + b["r2"][p, n].astype(F32)
    b["s3"][p] = total
    return [send(b["s3"].at[p], b["r4"].at[p], b["half_in"], p, device(at, hi=1 - at["hi"]))]


def scatter_total(at, p, b):
    return b["s3"][p] + b["r4"][p]


def gather_rows(at, p, modes, b):
    here = modes.at[p, at["core"], at["x"], at["y"], at["lo"]]
    return [
        send(here, here, b["rows_out"], p * len(STEPS) + n, device(at, **moved(at, step)))
        for n, step in enumerate(STEPS)
    ]


def gather_core(at, p, modes, b, copies):
    passed = []
    for dx in (0, 1, 3, 2):
        arrived([copy for copy, step in zip(copies, STEPS) if step[0] == dx])
        block = modes.at[p, at["core"], turned(at, "x", 4 - dx)]
        passed.append(send(block, block, b["core_out"], 4 * p + dx, device(at, core=1 - at["core"])))
    return passed


def exchange_scratch():
    pair = lambda n: [pltpu.SemaphoreType.DMA((n,)), pltpu.SemaphoreType.DMA((n,))]
    rows = len(STEPS)
    return dict(
        r1=pltpu.VMEM((X, 4, 4, 2, C, 2 * K), BF),
        s1=pltpu.VMEM((X, 4, 4, 2, C, 2 * K), BF),
        r2=pltpu.VMEM((X, rows, C, 2 * K), BF),
        s3=pltpu.VMEM((X, C, 2 * K), F32),
        r4=pltpu.VMEM((X, C, 2 * K), F32),
        core_in=pair(X),
        rows_in=pair(X * rows),
        half_in=pair(X),
        rows_out=pair(X * rows),
        core_out=pair(4 * X),
    )


def widen(v, table):
    hi, lo = split(v)
    return dot(hi, table) + dot(lo, table)


def narrow(v, table):
    hi, lo = split(v)
    return dot_nt(hi, table) + dot_nt(lo, table)


def put_modes(at, p, modes, real, imag):
    block = jnp.concatenate([real, imag], axis=0).T
    modes[p, at["core"], at["x"], at["y"], at["lo"]] = block.astype(BF)


def mix(at, p, total, w_all, over_o, over_i, modes, spec):
    t = total.T
    spec[p] = t
    s_real = widen(t[:K], over_o)
    s_imag = widen(t[K:], over_o)
    w_real, w_imag = w_all[:, : C * C].astype(F32), w_all[:, C * C :].astype(F32)
    real = narrow(w_real * s_real - w_imag * s_imag, over_i)
    imag = narrow(w_real * s_imag + w_imag * s_real, over_i)
    put_modes(at, p, modes, real, imag)


def unmix(at, p, total, w_all, over_o, over_i, modes, dual):
    t = total.T * 2.0
    dual[p] = t
    d_real = widen(t[:K], over_i)
    d_imag = widen(t[K:], over_i)
    w_real, w_imag = w_all[:, : C * C].astype(F32), w_all[:, C * C :].astype(F32)
    real = narrow(w_real * d_real + w_imag * d_imag, over_o)
    imag = narrow(w_real * d_imag - w_imag * d_real, over_o)
    put_modes(at, p, modes, real * 0.5, imag * 0.5)


def weight_gradient(at, spec, dual, over_o, over_i, grad):
    half = K // 2
    real, imag = 0.0, 0.0
    for p in range(X):
        top = pl.ds(pl.multiple_of(at["hi"] * half, half), half)
        low = pl.ds(pl.multiple_of(at["hi"] * half + K, half), half)
        s_real, s_imag = widen(spec[p, top], over_o), widen(spec[p, low], over_o)
        d_real, d_imag = widen(dual[p, top], over_i), widen(dual[p, low], over_i)
        real = real + d_real * s_real + d_imag * s_imag
        imag = imag + d_imag * s_real - d_real * s_imag
    grad[:, : C * C] = real
    grad[:, C * C :] = imag


def gelu_terms(v):
    e = jnp.exp(v * v * -0.5)
    t = 1.0 / (1.0 + jnp.abs(v) * (0.3275911 / math.sqrt(2.0)))
    q = t * (0.5 * 1.061405429) - 0.5 * 1.453152027
    q = q * t + 0.5 * 1.421413741
    q = q * t - 0.5 * 0.284496736
    q = q * t + 0.5 * 0.254829592
    q = q * t * e
    phi = jnp.where(v >= 0.0, 1.0 - q, q)
    return v * phi, phi + v * e * (1.0 / math.sqrt(2.0 * math.pi))


def group_masks():
    a = lax.broadcasted_iota(jnp.int32, (C * G, C * G), 0)
    b = lax.broadcasted_iota(jnp.int32, (C * G, C * G), 1)
    same = lax.rem(a, G) == lax.rem(b, G)
    m = lax.broadcasted_iota(jnp.int32, (C * G, C), 0)
    n = lax.broadcasted_iota(jnp.int32, (C * G, C), 1)
    over = (m // G == n).astype(F32).astype(BF)
    return same, over


def kron_of(half, over, same):
    return jnp.where(same, dot_nt(half.astype(BF), over), 0.0).astype(BF)


def pointwise(f_buf, kron, bias_col, base):
    for g in range(NG):
        f = f_buf[:, rows_of(g), :].reshape(C * G, COLS)
        base[g] = dot(kron[...], f) + bias_col[:, :1]


def pointwise_back(g_buf, kron, base):
    for g in range(NG):
        base[g] = dot(kron[...], g_buf[:, rows_of(g), :].reshape(C * G, COLS))


def layer(spread, base, cot, zi, zf, o_buf, g_buf, rows, between=None):
    pre, slope_of = {}, {}
    for s in range(NG + 2):
        if s < NG:
            pre[s] = dot(spread[:, rows_of(s), :].reshape(C * G, 4 * K), zi[...]) + base[s]
        if 1 <= s <= NG:
            at = rows_of(s - 1)
            value, slope = gelu_terms(pre.pop(s - 1))
            o_buf[:, at, :] = value.astype(BF).reshape(C, G, COLS)
            gp = (cot[:, at, :].reshape(C * G, COLS).astype(F32) * slope).astype(BF)
            g_buf[:, at, :] = gp.reshape(C, G, COLS)
            slope_of[s - 1] = gp
        if s >= 2:
            r = dot(slope_of.pop(s - 2), zf[...]).astype(BF)
            rows[:, rows_of(s - 2), :] = r.reshape(C, G, 4 * K)
        if between is not None and s == NG // 2:
            between()


def point_gradient(g_buf, f_buf, acc, bias_acc, first):
    total, sums = 0.0, 0.0
    for q in range(0, NG, 4):
        gs = [g_buf[:, rows_of(q + e), :].reshape(C * G, COLS) for e in range(4)]
        fs = [f_buf[:, rows_of(q + e), :].reshape(C * G, COLS) for e in range(4)]
        total = total + dot_nt(jnp.concatenate(gs, axis=1), jnp.concatenate(fs, axis=1))
        for gp in gs:
            gp = gp.astype(F32)
            sums = sums + gp[:, : COLS // 2] + gp[:, COLS // 2 :]
    acc[...] = total if first else acc[...] + total
    bias_acc[...] = sums if first else bias_acc[...] + sums


def main_kernel(
    field, cot, weights, zf_all, zi_all, yf_all, yi_all, point, bias, over_o_ref, over_i_ref,
    out, base, modes2, grad, zi, yi, small_out,
    f_buf, c_buf, spread, rows, g_buf, wide, part, modes, part2,
    zf, yf, kron, kron_back, bias_col, acc, bias_acc, w_all, spec, dual, s_small, r_small,
    b1, b2, sems, w_sems, small_sems,
):
    at = places()
    gy, gz = lax.axis_index("gy"), lax.axis_index("gz")
    local = pltpu.make_async_copy
    half = C // 2
    loads = [
        local(field.at[:half, 0], f_buf.at[0, :half], sems.at[0]),
        local(zf_all.at[gz], zf, sems.at[1]),
        local(field.at[half:, 0], f_buf.at[0, half:], sems.at[2]),
        local(yf_all.at[gy], yf, sems.at[3]),
        local(field.at[:, 1], f_buf.at[1], sems.at[4]),
        local(weights, w_all.at[at["hi"]], sems.at[5]),
        local(zi_all.at[gz], zi, sems.at[6]),
        local(yi_all.at[gy], yi, sems.at[7]),
        local(cot.at[:, 0], c_buf.at[0], sems.at[8]),
        local(cot.at[:, 1], c_buf.at[1], sems.at[9]),
    ]
    for load in loads[:5]:
        load.start()
    barrier, partners = greet(at)

    loads[0].wait()
    loads[1].wait()
    forward_z(f_buf.at[0], zf, rows.at[0], 0, half)
    loads[2].wait()
    forward_z(f_buf.at[0], zf, rows.at[0], half, C)
    loads[3].wait()
    forward_y(rows.at[0], yf, wide.at[0], part.at[0])
    pl.semaphore_wait(barrier, partners)
    f0 = scatter_core(at, 0, part, b1)
    loads[4].wait()
    for load in loads[5:]:
        load.start()
    forward_z(f_buf.at[1], zf, rows.at[1], 0, C)
    arrived(f0)
    f0 = scatter_rows(at, 0, part, b1)
    forward_y(rows.at[1], yf, wide.at[1], part.at[1])
    f1 = scatter_core(at, 1, part, b1)
    w_there = pltpu.make_async_remote_copy(
        src_ref=weights,
        dst_ref=w_all.at[at["hi"]],
        send_sem=w_sems.at[0],
        recv_sem=w_sems.at[1],
        device_id=device(at, hi=1 - at["hi"]),
        device_id_type=MESH,
    )
    w_there.start()
    same, over = group_masks()
    kron[...] = kron_of(dot(over, point[...]), over, same)
    bias_wide = jnp.broadcast_to(bias[...].astype(F32), (2 * K, C)).astype(BF)
    bias_col[...] = dot_nt(over, bias_wide)
    over_o, over_i = over_o_ref[...], over_i_ref[...]
    arrived(f1)
    f1 = scatter_rows(at, 1, part, b1)
    pointwise(f_buf.at[0], kron, bias_col, base.at[0])
    arrived(f0)
    f0 = scatter_halves(at, 0, b1)
    pointwise(f_buf.at[1], kron, bias_col, base.at[1])
    for load in loads[5:]:
        load.wait()
    w_there.wait()
    w = w_all[...].reshape(K, 2 * C * C)
    arrived(f0)
    mix(at, 0, scatter_total(at, 0, b1), w, over_o, over_i, modes, spec)
    f0 = gather_rows(at, 0, modes, b1)
    arrived(f1)
    f1 = scatter_halves(at, 1, b1)
    kron_back[...] = kron_of(dot_nt(over, point[...]), over, same)
    arrived(f1)
    mix(at, 1, scatter_total(at, 1, b1), w, over_o, over_i, modes, spec)
    f1 = gather_rows(at, 1, modes, b1)
    f0 = gather_core(at, 0, modes, b1, f0)

    arrived(f0)
    inverse_y(modes.at[0], yi, wide.at[0], spread.at[0])
    passed = []
    layer(
        spread.at[0], base.at[0], c_buf.at[0], zi, zf, out.at[0], g_buf.at[0], rows.at[0],
        lambda: passed.extend(gather_core(at, 1, modes, b1, f1)),
    )
    forward_y(rows.at[0], yf, wide.at[0], part2.at[0])
    f0 = scatter_core(at, 0, part2, b2)
    arrived(passed)
    inverse_y(modes.at[1], yi, wide.at[1], spread.at[1])
    arrived(f0)
    f0 = scatter_rows(at, 0, part2, b2)
    layer(spread.at[1], base.at[1], c_buf.at[1], zi, zf, out.at[1], g_buf.at[1], rows.at[1])
    forward_y(rows.at[1], yf, wide.at[1], part2.at[1])
    f1 = scatter_core(at, 1, part2, b2)
    arrived(f0)
    f0 = scatter_halves(at, 0, b2)
    arrived(f1)
    f1 = scatter_rows(at, 1, part2, b2)

    point_gradient(g_buf.at[0], f_buf.at[0], acc, bias_acc, True)
    arrived(f0)
    unmix(at, 0, scatter_total(at, 0, b2), w, over_o, over_i, modes2, dual)
    f0 = gather_rows(at, 0, modes2, b2)
    point_gradient(g_buf.at[1], f_buf.at[1], acc, bias_acc, False)
    kept = jnp.where(same, acc[...], 0.0).reshape(C, G, C * G).sum(axis=1)
    term = jnp.dot(kept, over.astype(F32), precision=lax.Precision.HIGHEST)
    total = bias_acc[...].reshape(C, G, COLS // 2).sum(axis=1).sum(axis=1, keepdims=True)
    s_small[0, :8] = fold(term)
    s_small[0, 8:] = fold(jnp.broadcast_to(total, (C, C)))
    arrived(f1)
    f1 = scatter_halves(at, 1, b2)
    small = [
        send(s_small.at[0], r_small.at[n], small_sems, n, to) for n, to in enumerate(across(at))
    ]
    pointwise_back(g_buf.at[0], kron_back, base.at[0])
    arrived(f1)
    unmix(at, 1, scatter_total(at, 1, b2), w, over_o, over_i, modes2, dual)
    f1 = gather_rows(at, 1, modes2, b2)
    arrived(small)
    s_small[1] = s_small[0] + r_small[0] + r_small[1] + r_small[2]
    small = [
        send(s_small.at[1], r_small.at[3 + n], small_sems, 3 + n, device(at, **moved(at, step)))
        for n, step in enumerate(STEPS)
    ]
    f0 = gather_core(at, 0, modes2, b2, f0)
    weight_gradient(at, spec, dual, over_o, over_i, grad)
    pointwise_back(g_buf.at[1], kron_back, base.at[1])
    arrived(f0)
    f1 = gather_core(at, 1, modes2, b2, f1)
    arrived(small)
    total = s_small[1]
    for n in range(len(STEPS)):
        total = total + r_small[3 + n]
    small_out[...] = total * (1.0 / math.sqrt(X * Y * Z))
    arrived(f1)


def last_kernel(
    held, base, modes, grad_in, zi, yi, small,
    out, output, grad, term, total, spread, o_buf, wide, out_sems,
):
    local = pltpu.make_async_copy
    outs = [local(held.at[x], output.at[:, x], out_sems.at[x]) for x in range(X)]
    outs.append(local(grad_in, grad, out_sems.at[2]))
    for copy in outs:
        copy.start()
    term[...] = unfold(small[:8])
    total[...] = unfold(small[8:]).T[:1]
    for x in range(X):
        inverse_y(modes.at[x], yi, wide.at[x], spread.at[x])
        for g in range(NG):
            at = rows_of(g)
            v = dot(spread[x, :, at, :].reshape(C * G, 4 * K), zi[...]) + base[x, g]
            o_buf[x, :, at, :] = v.astype(BF).reshape(C, G, COLS)
        outs.append(local(o_buf.at[x], out.at[:, x], out_sems.at[3 + x]))
        outs[-1].start()
    for copy in outs:
        copy.wait()


VMEM = pl.BlockSpec(memory_space=pltpu.VMEM)
ANY = pl.BlockSpec(memory_space=pl.ANY)


def params(mib, collective_id=None):
    limit = mib * 1024 * 1024
    if collective_id is None:
        return pltpu.CompilerParams(vmem_limit_bytes=limit)
    return pltpu.CompilerParams(
        vmem_limit_bytes=limit, collective_id=collective_id, has_side_effects=True
    )


def grid_buffer(dtype=BF):
    return pltpu.VMEM((X, C, ROWS, COLS), dtype)


def local(field, spec_weight, point_weight, bias, cotangent):
    zf, zi, yf, yi = (jnp.asarray(t) for t in make_tables())
    over_o, over_i = (jnp.asarray(t) for t in make_spreads())
    shape = jax.ShapeDtypeStruct
    deep = (X, 2, 4, 4, 2, C, 2 * K)
    lines = pltpu.VMEM((X, C, ROWS, 4 * K), BF)
    wide = pltpu.VMEM((X, K * C, 2 * K), F32)
    table = pltpu.VMEM((COLS, COLS), BF)
    vmem = pltpu.VMEM
    dma = pltpu.SemaphoreType.DMA
    square = (C * G, C * G)

    held, base, modes, grad_spec, zi, yi, small = pl.pallas_call(
        main_kernel,
        out_shape=(
            grid_buffer(),
            vmem((X, NG, C * G, COLS), F32),
            vmem(deep, BF),
            vmem((K // 2, 2 * C * C), F32),
            table,
            vmem((2 * ROWS, K), BF),
            vmem((16, 4 * C), F32),
        ),
        in_specs=[ANY] * 7 + [VMEM] * 4,
        out_specs=[VMEM] * 7,
        scratch_shapes=[
            grid_buffer(), grid_buffer(), lines, lines, grid_buffer(),
            wide, vmem(deep, BF), vmem(deep, BF), vmem(deep, BF),
            table, vmem((K, 2 * ROWS), BF),
            vmem(square, BF), vmem(square, BF), vmem((C * G, 2 * K), F32), vmem(square, F32),
            vmem((C * G, COLS // 2), F32),
            vmem((2, K // 2, 2 * C * C), BF),
            vmem((X, 2 * K, C), F32), vmem((X, 2 * K, C), F32),
            vmem((2, 16, 4 * C), F32), vmem((3 + len(STEPS), 16, 4 * C), F32),
            exchange_scratch(), exchange_scratch(),
            dma((10,)), dma((2,)), [dma((3 + len(STEPS),)), dma((3 + len(STEPS),))],
        ],
        compiler_params=params(46, 1),
        name="layer",
    )(
        field, cotangent, spec_weight, zf, zi, yf, yi,
        point_weight, bias.reshape(1, C), over_o, over_i,
    )

    grad_input, output, grad, term, total = pl.pallas_call(
        last_kernel,
        out_shape=(
            shape(field.shape, BF),
            shape(field.shape, BF),
            shape(grad_spec.shape, F32),
            shape((C, C), F32),
            shape((1, C), F32),
        ),
        in_specs=[VMEM] * 7,
        out_specs=[ANY] * 3 + [VMEM] * 2,
        scratch_shapes=[lines, grid_buffer(), wide, dma((5,))],
        compiler_params=params(24),
        name="input_gradient",
    )(held, base, modes, grad_spec, zi, yi, small)

    return output, grad_input, grad, term, total.reshape(C)


def solution(mesh):
    grid = P(None, None, "gy", "gz")
    owned = P(("gy", "gz"), None)
    return jax.shard_map(
        local,
        mesh=mesh,
        in_specs=(grid, owned, P(), P(), grid),
        out_specs=(grid, grid, owned, P(), P()),
        check_vma=False,
    )
```

```python
import functools
import math

import jax
import jax.numpy as jnp
import numpy as np
from jax import lax
from jax.experimental import pallas as pl
from jax.experimental.pallas import tpu as pltpu

P = jax.sharding.PartitionSpec
BF = jnp.bfloat16
F32 = jnp.float32

C = 32
X = 2
Y = 2048
Z = 2048
K = 64
ROWS = 128
COLS = 256
G = 16
NG = ROWS // G

MESH = pl.DeviceIdType.MESH


def row_order():
    order = []
    for core in range(2):
        for cx in range(4):
            for cy in range(4):
                for lo in range(2):
                    order.append(cx * 16 + lo * 8 + core * 4 + cy)
    return np.array(order)


def make_tables():
    j = row_order()
    fy = np.where(j < K // 2, j, Y - K + j)
    y = np.arange(Y)
    ang_y = 2.0 * np.pi * ((fy[:, None] * y[None, :]) % Y) / Y
    z = np.arange(Z)
    ang_z = 2.0 * np.pi * ((np.arange(K)[:, None] * z[None, :]) % Z) / Z
    cy, sy = np.cos(ang_y), np.sin(ang_y)
    cz, sz = np.cos(ang_z), np.sin(ang_z)
    zf = np.concatenate([cz, -sz, -sz, -cz], axis=0)
    zf = zf.reshape(4 * K, Z // COLS, COLS).transpose(1, 0, 2)
    yf = np.stack([cy, sy], axis=0).reshape(2, K, Y // ROWS, ROWS)
    yf = yf.transpose(2, 1, 0, 3).reshape(Y // ROWS, K, 2 * ROWS)
    yi = np.stack([cy, sy], axis=0).reshape(2, K, Y // ROWS, ROWS)
    yi = yi.transpose(2, 0, 3, 1).reshape(Y // ROWS, 2 * ROWS, K)
    bf = lambda a: np.ascontiguousarray(a).astype(jnp.bfloat16)
    scale = 1.0 / math.sqrt(Y * Z)
    return (
        bf(zf.transpose(0, 2, 1)),
        bf(zf),
        bf(yf * scale),
        bf(yi * (2.0 * scale)),
    )


def make_spreads():
    lane = np.arange(C * C)
    rows = np.arange(C)[:, None]
    over_o = (lane[None, :] // C == rows).astype(np.float32)
    over_i = (lane[None, :] % C == rows).astype(np.float32)
    return over_o.astype(jnp.bfloat16), over_i.astype(jnp.bfloat16)


def dot(a, b):
    return jnp.dot(a, b, preferred_element_type=F32)


def dot_nt(a, b):
    return lax.dot_general(a, b, (((1,), (1,)), ((), ())), preferred_element_type=F32)


def split(v):
    hi = v.astype(BF)
    return hi, (v - hi.astype(F32)).astype(BF)


def forward_z(src, zf, rows, begin, end):
    for c in range(begin, end, 4):
        f = src[pl.ds(c, 4)].reshape(4 * ROWS, COLS)
        rows[pl.ds(c, 4)] = dot(f, zf[...]).astype(BF).reshape(4, ROWS, 4 * K)


def forward_y(rows, yf, wide, part):
    for c in range(0, C, 2):
        one, two = rows[c], rows[c + 1]
        upper = jnp.concatenate([one[:, : 2 * K], two[:, : 2 * K]], axis=1)
        lower = jnp.concatenate([one[:, 2 * K :], two[:, 2 * K :]], axis=1)
        r = dot(yf[...], jnp.concatenate([upper, lower], axis=0))
        wide[pl.ds(c, K, stride=C), :] = r[:, : 2 * K]
        wide[pl.ds(c + 1, K, stride=C), :] = r[:, 2 * K :]
    step = K * C // 8
    for n in range(8):
        part[n // 4, n % 4] = wide[pl.ds(n * step, step), :].astype(BF).reshape(4, 2, C, 2 * K)


def inverse_y(modes, yi, wide, spread):
    step = K * C // 8
    for n in range(8):
        wide[pl.ds(n * step, step), :] = modes[n // 4, n % 4].astype(F32).reshape(step, 2 * K)
    for c in range(0, C, 2):
        one = wide[pl.ds(c, K, stride=C), :].astype(BF)
        two = wide[pl.ds(c + 1, K, stride=C), :].astype(BF)
        r = dot(yi[...], jnp.concatenate([one, two], axis=1)).astype(BF)
        for e in range(2):
            lanes = slice(e * 2 * K, (e + 1) * 2 * K)
            spread[c + e, :, : 2 * K] = r[:ROWS, lanes]
            spread[c + e, :, 2 * K :] = r[ROWS:, lanes]


def fold(v):
    return jnp.concatenate([v[8 * n : 8 * n + 8] for n in range(C // 8)], axis=1)


def unfold(v):
    return jnp.concatenate([v[:, C * n : C * n + C] for n in range(C // 8)], axis=0)


def rows_of(g):
    return pl.ds(g * G, G)


def places():
    gy, gz = lax.axis_index("gy"), lax.axis_index("gz")
    return dict(x=gy // 4, lo=gy // 2 % 2, core=gy % 2, y=gz // 2, hi=gz % 2)


def device(at, **other):
    at = dict(at, **other)
    return {
        "gy": at["x"] * 4 + at["lo"] * 2 + at["core"],
        "gz": at["y"] * 2 + at["hi"],
    }


def turned(at, axis, step):
    return lax.rem(at[axis] + step, 4)


STEPS = [(dx, dy, dl) for dx in (2, 1, 3, 0) for dy in (2, 1, 3, 0) for dl in (1, 0)][:-1]


def moved(at, step):
    dx, dy, dl = step
    lo = 1 - at["lo"] if dl else at["lo"]
    return dict(x=turned(at, "x", dx), y=turned(at, "y", dy), lo=lo)


def across(at):
    core, hi = 1 - at["core"], 1 - at["hi"]
    return [device(at, core=core), device(at, hi=hi), device(at, core=core, hi=hi)]


def greet(at):
    barrier = pltpu.get_barrier_semaphore()
    partners = across(at) + [device(at, **moved(at, step)) for step in STEPS]
    for partner in partners:
        pl.semaphore_signal(barrier, inc=1, device_id=partner, device_id_type=MESH)
    return barrier, len(partners)


def send(src, dst, sems, n, to):
    send_sem, recv_sem = sems
    copy = pltpu.make_async_remote_copy(
        src_ref=src,
        dst_ref=dst,
        send_sem=send_sem.at[n],
        recv_sem=recv_sem.at[n],
        device_id=to,
        device_id_type=MESH,
    )
    copy.start()
    return copy


def arrived(copies):
    for copy in copies:
        copy.wait()


def scatter_core(at, p, part, b):
    other = 1 - at["core"]
    return [send(part.at[p, other], b["r1"].at[p], b["core_in"], p, device(at, core=other))]


def scatter_rows(at, p, part, b):
    me = at["core"]
    for cx in range(4):
        b["s1"][p, cx] = (part[p, me, cx].astype(F32) + b["r1"][p, cx].astype(F32)).astype(BF)
    copies = []
    for n, step in enumerate(STEPS):
        to = moved(at, step)
        copies.append(
            send(
                b["s1"].at[p, to["x"], to["y"], to["lo"]],
                b["r2"].at[p, n],
                b["rows_in"],
                p * len(STEPS) + n,
                device(at, **to),
            )
        )
    return copies


def scatter_halves(at, p, b):
    total = b["s1"][p, at["x"], at["y"], at["lo"]].astype(F32)
    for n in range(len(STEPS)):
        total = total + b["r2"][p, n].astype(F32)
    b["s3"][p] = total
    return [send(b["s3"].at[p], b["r4"].at[p], b["half_in"], p, device(at, hi=1 - at["hi"]))]


def scatter_total(at, p, b):
    return b["s3"][p] + b["r4"][p]


def gather_rows(at, p, modes, b):
    here = modes.at[p, at["core"], at["x"], at["y"], at["lo"]]
    return [
        send(here, here, b["rows_out"], p * len(STEPS) + n, device(at, **moved(at, step)))
        for n, step in enumerate(STEPS)
    ]


def gather_core(at, p, modes, b, copies):
    passed = []
    for dx in (0, 1, 3, 2):
        arrived([copy for copy, step in zip(copies, STEPS) if step[0] == dx])
        block = modes.at[p, at["core"], turned(at, "x", 4 - dx)]
        passed.append(send(block, block, b["core_out"], 4 * p + dx, device(at, core=1 - at["core"])))
    return passed


def exchange_scratch():
    pair = lambda n: [pltpu.SemaphoreType.DMA((n,)), pltpu.SemaphoreType.DMA((n,))]
    rows = len(STEPS)
    return dict(
        r1=pltpu.VMEM((X, 4, 4, 2, C, 2 * K), BF),
        s1=pltpu.VMEM((X, 4, 4, 2, C, 2 * K), BF),
        r2=pltpu.VMEM((X, rows, C, 2 * K), BF),
        s3=pltpu.VMEM((X, C, 2 * K), F32),
        r4=pltpu.VMEM((X, C, 2 * K), F32),
        core_in=pair(X),
        rows_in=pair(X * rows),
        half_in=pair(X),
        rows_out=pair(X * rows),
        core_out=pair(4 * X),
    )


def widen(v, table):
    hi, lo = split(v)
    return dot(hi, table) + dot(lo, table)


def narrow(v, table):
    hi, lo = split(v)
    return dot_nt(hi, table) + dot_nt(lo, table)


def put_modes(at, p, modes, real, imag):
    block = jnp.concatenate([real, imag], axis=0).T
    modes[p, at["core"], at["x"], at["y"], at["lo"]] = block.astype(BF)


def mix(at, p, total, w_all, over_o, over_i, modes, spec):
    t = total.T
    spec[p] = t
    s_real = widen(t[:K], over_o)
    s_imag = widen(t[K:], over_o)
    w_real, w_imag = w_all[:, : C * C].astype(F32), w_all[:, C * C :].astype(F32)
    real = narrow(w_real * s_real - w_imag * s_imag, over_i)
    imag = narrow(w_real * s_imag + w_imag * s_real, over_i)
    put_modes(at, p, modes, real, imag)


def unmix(at, p, total, w_all, over_o, over_i, modes, dual):
    t = total.T * 2.0
    dual[p] = t
    d_real = widen(t[:K], over_i)
    d_imag = widen(t[K:], over_i)
    w_real, w_imag = w_all[:, : C * C].astype(F32), w_all[:, C * C :].astype(F32)
    real = narrow(w_real * d_real + w_imag * d_imag, over_o)
    imag = narrow(w_real * d_imag - w_imag * d_real, over_o)
    put_modes(at, p, modes, real * 0.5, imag * 0.5)


def weight_gradient(at, spec, dual, over_o, over_i, grad):
    half = K // 2
    real, imag = 0.0, 0.0
    for p in range(X):
        top = pl.ds(pl.multiple_of(at["hi"] * half, half), half)
        low = pl.ds(pl.multiple_of(at["hi"] * half + K, half), half)
        s_real, s_imag = widen(spec[p, top], over_o), widen(spec[p, low], over_o)
        d_real, d_imag = widen(dual[p, top], over_i), widen(dual[p, low], over_i)
        real = real + d_real * s_real + d_imag * s_imag
        imag = imag + d_imag * s_real - d_real * s_imag
    grad[:, : C * C] = real
    grad[:, C * C :] = imag


def gelu_terms(v):
    phi = 0.5 + 0.5 * lax.erf(v * math.sqrt(0.5))
    return v * phi, phi + v * jnp.exp(v * v * -0.5) * (1.0 / math.sqrt(2.0 * math.pi))


def group_masks():
    a = lax.broadcasted_iota(jnp.int32, (C * G, C * G), 0)
    b = lax.broadcasted_iota(jnp.int32, (C * G, C * G), 1)
    same = ((a ^ b) & (G - 1)) == 0
    m = lax.broadcasted_iota(jnp.int32, (C * G, C), 0)
    n = lax.broadcasted_iota(jnp.int32, (C * G, C), 1)
    over = (m - n * G).astype(F32)
    over = jnp.where((over >= 0.0) & (over < float(G)), 1.0, 0.0).astype(BF)
    return same, over


def kron_of(half, over, same):
    return jnp.where(same, dot_nt(half.astype(BF), over), 0.0).astype(BF)


def pointwise(f_buf, kron, bias_col, base):
    for g in range(NG):
        f = f_buf[:, rows_of(g), :].reshape(C * G, COLS)
        base[g] = dot(kron[...], f) + bias_col[:, :1]


def pointwise_back(g_buf, kron, base):
    for g in range(NG):
        base[g] = dot(kron[...], g_buf[:, rows_of(g), :].reshape(C * G, COLS))


def layer(spread, base, cot, zi, zf, o_buf, g_buf, rows):
    pre, slope_of = {}, {}
    for s in range(NG + 2):
        if s < NG:
            pre[s] = dot(spread[:, rows_of(s), :].reshape(C * G, 4 * K), zi[...]) + base[s]
        if 1 <= s <= NG:
            at = rows_of(s - 1)
            value, slope = gelu_terms(pre.pop(s - 1))
            o_buf[:, at, :] = value.astype(BF).reshape(C, G, COLS)
            gp = (cot[:, at, :].reshape(C * G, COLS).astype(F32) * slope).astype(BF)
            g_buf[:, at, :] = gp.reshape(C, G, COLS)
            slope_of[s - 1] = gp
        if s >= 2:
            r = dot(slope_of.pop(s - 2), zf[...]).astype(BF)
            rows[:, rows_of(s - 2), :] = r.reshape(C, G, 4 * K)


def point_gradient(g_buf, f_buf, acc, bias_acc, first):
    total, sums = 0.0, 0.0
    for q in range(0, NG, 4):
        gs = [g_buf[:, rows_of(q + e), :].reshape(C * G, COLS) for e in range(4)]
        fs = [f_buf[:, rows_of(q + e), :].reshape(C * G, COLS) for e in range(4)]
        total = total + dot_nt(jnp.concatenate(gs, axis=1), jnp.concatenate(fs, axis=1))
        for gp in gs:
            gp = gp.astype(F32)
            sums = sums + gp[:, : COLS // 2] + gp[:, COLS // 2 :]
    acc[...] = total if first else acc[...] + total
    bias_acc[...] = sums if first else bias_acc[...] + sums


def main_kernel(
    field, cot, weights, zf_all, zi_all, yf_all, yi_all, point, bias, over_o_ref, over_i_ref,
    out, base, modes2, grad, zi, yi, small_out,
    f_buf, c_buf, spread, rows, g_buf, wide, part, modes, part2,
    zf, yf, kron, kron_back, bias_col, acc, bias_acc, w_all, spec, dual, s_small, r_small,
    b1, b2, sems, w_sems, small_sems,
):
    at = places()
    gy, gz = lax.axis_index("gy"), lax.axis_index("gz")
    local = pltpu.make_async_copy
    half = C // 2
    loads = [
        local(field.at[:half, 0], f_buf.at[0, :half], sems.at[0]),
        local(zf_all.at[gz], zf, sems.at[1]),
        local(field.at[half:, 0], f_buf.at[0, half:], sems.at[2]),
        local(yf_all.at[gy], yf, sems.at[3]),
        local(field.at[:, 1], f_buf.at[1], sems.at[4]),
        local(weights, w_all.at[at["hi"]], sems.at[5]),
        local(zi_all.at[gz], zi, sems.at[6]),
        local(yi_all.at[gy], yi, sems.at[7]),
        local(cot.at[:, 0], c_buf.at[0], sems.at[8]),
        local(cot.at[:, 1], c_buf.at[1], sems.at[9]),
    ]
    for load in loads[:5]:
        load.start()
    barrier, partners = greet(at)

    loads[0].wait()
    loads[1].wait()
    forward_z(f_buf.at[0], zf, rows.at[0], 0, half)
    loads[2].wait()
    forward_z(f_buf.at[0], zf, rows.at[0], half, C)
    loads[3].wait()
    forward_y(rows.at[0], yf, wide.at[0], part.at[0])
    pl.semaphore_wait(barrier, partners)
    f0 = scatter_core(at, 0, part, b1)
    w_there = pltpu.make_async_remote_copy(
        src_ref=weights,
        dst_ref=w_all.at[at["hi"]],
        send_sem=w_sems.at[0],
        recv_sem=w_sems.at[1],
        device_id=device(at, hi=1 - at["hi"]),
        device_id_type=MESH,
    )
    w_there.start()
    loads[4].wait()
    forward_z(f_buf.at[1], zf, rows.at[1], 0, C)
    arrived(f0)
    f0 = scatter_rows(at, 0, part, b1)
    forward_y(rows.at[1], yf, wide.at[1], part.at[1])
    f1 = scatter_core(at, 1, part, b1)
    same, over = group_masks()
    kron[...] = kron_of(dot(over, point[...]), over, same)
    bias_wide = jnp.broadcast_to(bias[...].astype(F32), (2 * K, C)).astype(BF)
    bias_col[...] = dot_nt(over, bias_wide)
    over_o, over_i = over_o_ref[...], over_i_ref[...]
    arrived(f1)
    f1 = scatter_rows(at, 1, part, b1)
    for load in loads[5:]:
        load.start()
    pointwise(f_buf.at[0], kron, bias_col, base.at[0])
    arrived(f0)
    f0 = scatter_halves(at, 0, b1)
    pointwise(f_buf.at[1], kron, bias_col, base.at[1])
    for load in loads[5:]:
        load.wait()
    w_there.wait()
    w = w_all[...].reshape(K, 2 * C * C)
    arrived(f0)
    mix(at, 0, scatter_total(at, 0, b1), w, over_o, over_i, modes, spec)
    f0 = gather_rows(at, 0, modes, b1)
    arrived(f1)
    f1 = scatter_halves(at, 1, b1)
    kron_back[...] = kron_of(dot_nt(over, point[...]), over, same)
    arrived(f1)
    mix(at, 1, scatter_total(at, 1, b1), w, over_o, over_i, modes, spec)
    f1 = gather_rows(at, 1, modes, b1)
    f0 = gather_core(at, 0, modes, b1, f0)

    arrived(f0)
    inverse_y(modes.at[0], yi, wide.at[0], spread.at[0])
    layer(spread.at[0], base.at[0], c_buf.at[0], zi, zf, out.at[0], g_buf.at[0], rows.at[0])
    f1 = gather_core(at, 1, modes, b1, f1)
    forward_y(rows.at[0], yf, wide.at[0], part2.at[0])
    f0 = scatter_core(at, 0, part2, b2)
    arrived(f1)
    inverse_y(modes.at[1], yi, wide.at[1], spread.at[1])
    arrived(f0)
    f0 = scatter_rows(at, 0, part2, b2)
    layer(spread.at[1], base.at[1], c_buf.at[1], zi, zf, out.at[1], g_buf.at[1], rows.at[1])
    forward_y(rows.at[1], yf, wide.at[1], part2.at[1])
    f1 = scatter_core(at, 1, part2, b2)

    point_gradient(g_buf.at[0], f_buf.at[0], acc, bias_acc, True)
    arrived(f1)
    f1 = scatter_rows(at, 1, part2, b2)
    arrived(f0)
    f0 = scatter_halves(at, 0, b2)
    point_gradient(g_buf.at[1], f_buf.at[1], acc, bias_acc, False)
    same, over = group_masks()
    kept = jnp.where(same, acc[...], 0.0).reshape(C, G, C * G).sum(axis=1)
    term = jnp.dot(kept, over.astype(F32), precision=lax.Precision.HIGHEST)
    total = bias_acc[...].reshape(C, G, COLS // 2).sum(axis=1).sum(axis=1, keepdims=True)
    s_small[0, :8] = fold(term)
    s_small[0, 8:] = fold(jnp.broadcast_to(total, (C, C)))
    small = [
        send(s_small.at[0], r_small.at[n], small_sems, n, to) for n, to in enumerate(across(at))
    ]
    arrived(f0)
    unmix(at, 0, scatter_total(at, 0, b2), w, over_o, over_i, modes2, dual)
    f0 = gather_rows(at, 0, modes2, b2)
    arrived(f1)
    f1 = scatter_halves(at, 1, b2)
    pointwise_back(g_buf.at[0], kron_back, base.at[0])
    arrived(small)
    s_small[1] = s_small[0] + r_small[0] + r_small[1] + r_small[2]
    arrived(f1)
    unmix(at, 1, scatter_total(at, 1, b2), w, over_o, over_i, modes2, dual)
    f1 = gather_rows(at, 1, modes2, b2)
    small = [
        send(s_small.at[1], r_small.at[3 + n], small_sems, 3 + n, device(at, **moved(at, step)))
        for n, step in enumerate(STEPS)
    ]
    f0 = gather_core(at, 0, modes2, b2, f0)
    weight_gradient(at, spec, dual, over_o, over_i, grad)
    pointwise_back(g_buf.at[1], kron_back, base.at[1])
    arrived(f0)
    f1 = gather_core(at, 1, modes2, b2, f1)
    arrived(small)
    total = s_small[1]
    for n in range(len(STEPS)):
        total = total + r_small[3 + n]
    small_out[...] = total * (1.0 / math.sqrt(X * Y * Z))
    arrived(f1)


def last_kernel(
    held, base, modes, grad_in, zi, yi, small,
    out, output, grad, term, total, spread, o_buf, wide, out_sems,
):
    local = pltpu.make_async_copy
    outs = [local(held.at[x], output.at[:, x], out_sems.at[x]) for x in range(X)]
    outs.append(local(grad_in, grad, out_sems.at[2]))
    for copy in outs:
        copy.start()
    term[...] = unfold(small[:8])
    total[...] = unfold(small[8:]).T[:1]
    for x in range(X):
        inverse_y(modes.at[x], yi, wide.at[x], spread.at[x])
        for g in range(NG):
            at = rows_of(g)
            v = dot(spread[x, :, at, :].reshape(C * G, 4 * K), zi[...]) + base[x, g]
            o_buf[x, :, at, :] = v.astype(BF).reshape(C, G, COLS)
        outs.append(local(o_buf.at[x], out.at[:, x], out_sems.at[3 + x]))
        outs[-1].start()
    for copy in outs:
        copy.wait()


VMEM = pl.BlockSpec(memory_space=pltpu.VMEM)
ANY = pl.BlockSpec(memory_space=pl.ANY)


def params(mib, collective_id=None):
    limit = mib * 1024 * 1024
    if collective_id is None:
        return pltpu.CompilerParams(vmem_limit_bytes=limit)
    return pltpu.CompilerParams(
        vmem_limit_bytes=limit, collective_id=collective_id, has_side_effects=True
    )


def grid_buffer(dtype=BF):
    return pltpu.VMEM((X, C, ROWS, COLS), dtype)


def local(field, spec_weight, point_weight, bias, cotangent):
    zf, zi, yf, yi = (jnp.asarray(t) for t in make_tables())
    over_o, over_i = (jnp.asarray(t) for t in make_spreads())
    shape = jax.ShapeDtypeStruct
    deep = (X, 2, 4, 4, 2, C, 2 * K)
    lines = pltpu.VMEM((X, C, ROWS, 4 * K), BF)
    wide = pltpu.VMEM((X, K * C, 2 * K), F32)
    table = pltpu.VMEM((COLS, COLS), BF)
    vmem = pltpu.VMEM
    dma = pltpu.SemaphoreType.DMA
    square = (C * G, C * G)

    held, base, modes, grad_spec, zi, yi, small = pl.pallas_call(
        main_kernel,
        out_shape=(
            grid_buffer(),
            vmem((X, NG, C * G, COLS), F32),
            vmem(deep, BF),
            vmem((K // 2, 2 * C * C), F32),
            table,
            vmem((2 * ROWS, K), BF),
            vmem((16, 4 * C), F32),
        ),
        in_specs=[ANY] * 7 + [VMEM] * 4,
        out_specs=[VMEM] * 7,
        scratch_shapes=[
            grid_buffer(), grid_buffer(), lines, lines, grid_buffer(),
            wide, vmem(deep, BF), vmem(deep, BF), vmem(deep, BF),
            table, vmem((K, 2 * ROWS), BF),
            vmem(square, BF), vmem(square, BF), vmem((C * G, 2 * K), F32), vmem(square, F32),
            vmem((C * G, COLS // 2), F32),
            vmem((2, K // 2, 2 * C * C), BF),
            vmem((X, 2 * K, C), F32), vmem((X, 2 * K, C), F32),
            vmem((2, 16, 4 * C), F32), vmem((3 + len(STEPS), 16, 4 * C), F32),
            exchange_scratch(), exchange_scratch(),
            dma((10,)), dma((2,)), [dma((3 + len(STEPS),)), dma((3 + len(STEPS),))],
        ],
        compiler_params=params(46, 1),
        name="layer",
    )(
        field, cotangent, spec_weight, zf, zi, yf, yi,
        point_weight, bias.reshape(1, C), over_o, over_i,
    )

    grad_input, output, grad, term, total = pl.pallas_call(
        last_kernel,
        out_shape=(
            shape(field.shape, BF),
            shape(field.shape, BF),
            shape(grad_spec.shape, F32),
            shape((C, C), F32),
            shape((1, C), F32),
        ),
        in_specs=[VMEM] * 7,
        out_specs=[ANY] * 3 + [VMEM] * 2,
        scratch_shapes=[lines, grid_buffer(), wide, dma((5,))],
        compiler_params=params(24),
        name="input_gradient",
    )(held, base, modes, grad_spec, zi, yi, small)

    return output, grad_input, grad, term, total.reshape(C)


def solution(mesh):
    grid = P(None, None, "gy", "gz")
    owned = P(("gy", "gz"), None)
    return jax.shard_map(
        local,
        mesh=mesh,
        in_specs=(grid, owned, P(), P(), grid),
        out_specs=(grid, grid, owned, P(), P()),
        check_vma=False,
    )
```

```python
import functools
import math

import jax
import jax.numpy as jnp
import numpy as np
from jax import lax
from jax.experimental import pallas as pl
from jax.experimental.pallas import tpu as pltpu

P = jax.sharding.PartitionSpec
BF = jnp.bfloat16
F32 = jnp.float32

C = 32
X = 2
Y = 2048
Z = 2048
K = 64
ROWS = 128
COLS = 256
G = 16
NG = ROWS // G

MESH = pl.DeviceIdType.MESH


def row_order():
    order = []
    for core in range(2):
        for cx in range(4):
            for cy in range(4):
                for lo in range(2):
                    order.append(cx * 16 + lo * 8 + core * 4 + cy)
    return np.array(order)


def make_tables():
    j = row_order()
    fy = np.where(j < K // 2, j, Y - K + j)
    y = np.arange(Y)
    ang_y = 2.0 * np.pi * ((fy[:, None] * y[None, :]) % Y) / Y
    z = np.arange(Z)
    ang_z = 2.0 * np.pi * ((np.arange(K)[:, None] * z[None, :]) % Z) / Z
    cy, sy = np.cos(ang_y), np.sin(ang_y)
    cz, sz = np.cos(ang_z), np.sin(ang_z)
    zf = np.concatenate([cz, -sz, -sz, -cz], axis=0)
    zf = zf.reshape(4 * K, Z // COLS, COLS).transpose(1, 0, 2)
    yf = np.stack([cy, sy], axis=0).reshape(2, K, Y // ROWS, ROWS)
    yf = yf.transpose(2, 1, 0, 3).reshape(Y // ROWS, K, 2 * ROWS)
    yi = np.stack([cy, sy], axis=0).reshape(2, K, Y // ROWS, ROWS)
    yi = yi.transpose(2, 0, 3, 1).reshape(Y // ROWS, 2 * ROWS, K)
    bf = lambda a: np.ascontiguousarray(a).astype(jnp.bfloat16)
    scale = 1.0 / math.sqrt(Y * Z)
    return (
        bf(zf.transpose(0, 2, 1)),
        bf(zf),
        bf(yf * scale),
        bf(yi * (2.0 * scale)),
    )


def make_spreads():
    lane = np.arange(C * C)
    rows = np.arange(C)[:, None]
    over_o = (lane[None, :] // C == rows).astype(np.float32)
    over_i = (lane[None, :] % C == rows).astype(np.float32)
    return over_o.astype(jnp.bfloat16), over_i.astype(jnp.bfloat16)


def dot(a, b):
    return jnp.dot(a, b, preferred_element_type=F32)


def dot_nt(a, b):
    return lax.dot_general(a, b, (((1,), (1,)), ((), ())), preferred_element_type=F32)


def split(v):
    hi = v.astype(BF)
    return hi, (v - hi.astype(F32)).astype(BF)


def forward_z(src, zf, rows, begin, end):
    for c in range(begin, end, 4):
        f = src[pl.ds(c, 4)].reshape(4 * ROWS, COLS)
        rows[pl.ds(c, 4)] = dot(f, zf[...]).astype(BF).reshape(4, ROWS, 4 * K)


def forward_y(rows, yf, wide, part):
    for c in range(0, C, 2):
        one, two = rows[c], rows[c + 1]
        upper = jnp.concatenate([one[:, : 2 * K], two[:, : 2 * K]], axis=1)
        lower = jnp.concatenate([one[:, 2 * K :], two[:, 2 * K :]], axis=1)
        r = dot(yf[...], jnp.concatenate([upper, lower], axis=0))
        wide[pl.ds(c, K, stride=C), :] = r[:, : 2 * K]
        wide[pl.ds(c + 1, K, stride=C), :] = r[:, 2 * K :]
    step = K * C // 8
    for n in range(8):
        part[n // 4, n % 4] = wide[pl.ds(n * step, step), :].astype(BF).reshape(4, 2, C, 2 * K)


def inverse_y(modes, yi, wide, spread):
    step = K * C // 8
    for n in range(8):
        wide[pl.ds(n * step, step), :] = modes[n // 4, n % 4].astype(F32).reshape(step, 2 * K)
    for c in range(0, C, 2):
        one = wide[pl.ds(c, K, stride=C), :].astype(BF)
        two = wide[pl.ds(c + 1, K, stride=C), :].astype(BF)
        r = dot(yi[...], jnp.concatenate([one, two], axis=1)).astype(BF)
        for e in range(2):
            lanes = slice(e * 2 * K, (e + 1) * 2 * K)
            spread[c + e, :, : 2 * K] = r[:ROWS, lanes]
            spread[c + e, :, 2 * K :] = r[ROWS:, lanes]


def fold(v):
    return jnp.concatenate([v[8 * n : 8 * n + 8] for n in range(C // 8)], axis=1)


def unfold(v):
    return jnp.concatenate([v[:, C * n : C * n + C] for n in range(C // 8)], axis=0)


def rows_of(g):
    return pl.ds(g * G, G)


def places():
    gy, gz = lax.axis_index("gy"), lax.axis_index("gz")
    return dict(x=gy // 4, lo=gy // 2 % 2, core=gy % 2, y=gz // 2, hi=gz % 2)


def device(at, **other):
    at = dict(at, **other)
    return {
        "gy": at["x"] * 4 + at["lo"] * 2 + at["core"],
        "gz": at["y"] * 2 + at["hi"],
    }


def turned(at, axis, step):
    return lax.rem(at[axis] + step, 4)


STEPS = [(dx, dy, dl) for dx in (2, 1, 3, 0) for dy in (2, 1, 3, 0) for dl in (1, 0)][:-1]


def moved(at, step):
    dx, dy, dl = step
    lo = 1 - at["lo"] if dl else at["lo"]
    return dict(x=turned(at, "x", dx), y=turned(at, "y", dy), lo=lo)


def across(at):
    core, hi = 1 - at["core"], 1 - at["hi"]
    return [device(at, core=core), device(at, hi=hi), device(at, core=core, hi=hi)]


def greet(at):
    barrier = pltpu.get_barrier_semaphore()
    partners = across(at) + [device(at, **moved(at, step)) for step in STEPS]
    for partner in partners:
        pl.semaphore_signal(barrier, inc=1, device_id=partner, device_id_type=MESH)
    return barrier, len(partners)


def send(src, dst, sems, n, to):
    send_sem, recv_sem = sems
    copy = pltpu.make_async_remote_copy(
        src_ref=src,
        dst_ref=dst,
        send_sem=send_sem.at[n],
        recv_sem=recv_sem.at[n],
        device_id=to,
        device_id_type=MESH,
    )
    copy.start()
    return copy


def arrived(copies):
    for copy in copies:
        copy.wait()


def scatter_core(at, p, part, b):
    other = 1 - at["core"]
    return [send(part.at[p, other], b["r1"].at[p], b["core_in"], p, device(at, core=other))]


def scatter_rows(at, p, part, b):
    me = at["core"]
    copies = []
    for dx in (2, 1, 3, 0):
        cx = turned(at, "x", dx)
        b["s1"][p, cx] = (part[p, me, cx].astype(F32) + b["r1"][p, cx].astype(F32)).astype(BF)
        for n, step in enumerate(STEPS):
            if step[0] == dx:
                to = moved(at, step)
                copies.append(
                    send(
                        b["s1"].at[p, cx, to["y"], to["lo"]],
                        b["r2"].at[p, n],
                        b["rows_in"],
                        p * len(STEPS) + n,
                        device(at, **to),
                    )
                )
    return copies


def scatter_halves(at, p, b):
    total = b["s1"][p, at["x"], at["y"], at["lo"]].astype(F32)
    for n in range(len(STEPS)):
        total = total + b["r2"][p, n].astype(F32)
    b["s3"][p] = total
    return [send(b["s3"].at[p], b["r4"].at[p], b["half_in"], p, device(at, hi=1 - at["hi"]))]


def scatter_total(at, p, b):
    return b["s3"][p] + b["r4"][p]


def gather_rows(at, p, modes, b):
    here = modes.at[p, at["core"], at["x"], at["y"], at["lo"]]
    return [
        send(here, here, b["rows_out"], p * len(STEPS) + n, device(at, **moved(at, step)))
        for n, step in enumerate(STEPS)
    ]


def gather_core(at, p, modes, b, copies):
    passed = []
    for dx in (0, 1, 3, 2):
        arrived([copy for copy, step in zip(copies, STEPS) if step[0] == dx])
        block = modes.at[p, at["core"], turned(at, "x", 4 - dx)]
        passed.append(send(block, block, b["core_out"], 4 * p + dx, device(at, core=1 - at["core"])))
    return passed


def exchange_scratch():
    pair = lambda n: [pltpu.SemaphoreType.DMA((n,)), pltpu.SemaphoreType.DMA((n,))]
    rows = len(STEPS)
    return dict(
        r1=pltpu.VMEM((X, 4, 4, 2, C, 2 * K), BF),
        s1=pltpu.VMEM((X, 4, 4, 2, C, 2 * K), BF),
        r2=pltpu.VMEM((X, rows, C, 2 * K), BF),
        s3=pltpu.VMEM((X, C, 2 * K), F32),
        r4=pltpu.VMEM((X, C, 2 * K), F32),
        core_in=pair(X),
        rows_in=pair(X * rows),
        half_in=pair(X),
        rows_out=pair(X * rows),
        core_out=pair(4 * X),
    )


def widen(v, table):
    hi, lo = split(v)
    return dot(hi, table) + dot(lo, table)


def narrow(v, table):
    hi, lo = split(v)
    return dot_nt(hi, table) + dot_nt(lo, table)


def put_modes(at, p, modes, real, imag):
    block = jnp.concatenate([real, imag], axis=0).T
    modes[p, at["core"], at["x"], at["y"], at["lo"]] = block.astype(BF)


def mix(at, p, total, w_all, over_o, over_i, modes, spec):
    t = total.T
    spec[p] = t
    s_real = widen(t[:K], over_o)
    s_imag = widen(t[K:], over_o)
    w_real, w_imag = w_all[:, : C * C].astype(F32), w_all[:, C * C :].astype(F32)
    real = narrow(w_real * s_real - w_imag * s_imag, over_i)
    imag = narrow(w_real * s_imag + w_imag * s_real, over_i)
    put_modes(at, p, modes, real, imag)


def unmix(at, p, total, w_all, over_o, over_i, modes, dual):
    t = total.T * 2.0
    dual[p] = t
    d_real = widen(t[:K], over_i)
    d_imag = widen(t[K:], over_i)
    w_real, w_imag = w_all[:, : C * C].astype(F32), w_all[:, C * C :].astype(F32)
    real = narrow(w_real * d_real + w_imag * d_imag, over_o)
    imag = narrow(w_real * d_imag - w_imag * d_real, over_o)
    put_modes(at, p, modes, real * 0.5, imag * 0.5)


def weight_gradient(at, spec, dual, over_o, over_i, grad):
    half = K // 2
    real, imag = 0.0, 0.0
    for p in range(X):
        top = pl.ds(pl.multiple_of(at["hi"] * half, half), half)
        low = pl.ds(pl.multiple_of(at["hi"] * half + K, half), half)
        s_real, s_imag = widen(spec[p, top], over_o), widen(spec[p, low], over_o)
        d_real, d_imag = widen(dual[p, top], over_i), widen(dual[p, low], over_i)
        real = real + d_real * s_real + d_imag * s_imag
        imag = imag + d_imag * s_real - d_real * s_imag
    grad[:, : C * C] = real
    grad[:, C * C :] = imag


def gelu_terms(v):
    phi = 0.5 + 0.5 * lax.erf(v * math.sqrt(0.5))
    return v * phi, phi + v * jnp.exp(v * v * -0.5) * (1.0 / math.sqrt(2.0 * math.pi))


def group_masks():
    a = lax.broadcasted_iota(jnp.int32, (C * G, C * G), 0)
    b = lax.broadcasted_iota(jnp.int32, (C * G, C * G), 1)
    same = ((a ^ b) & (G - 1)) == 0
    m = lax.broadcasted_iota(jnp.int32, (C * G, C), 0)
    n = lax.broadcasted_iota(jnp.int32, (C * G, C), 1)
    over = (m - n * G).astype(F32)
    over = jnp.where((over >= 0.0) & (over < float(G)), 1.0, 0.0).astype(BF)
    return same, over


def kron_of(half, over, same):
    return jnp.where(same, dot_nt(half.astype(BF), over), 0.0).astype(BF)


def pointwise(f_buf, kron, bias_col, base):
    for g in range(NG):
        f = f_buf[:, rows_of(g), :].reshape(C * G, COLS)
        base[g] = dot(kron[...], f) + bias_col[:, :1]


def pointwise_back(g_buf, kron, base):
    for g in range(NG):
        base[g] = dot(kron[...], g_buf[:, rows_of(g), :].reshape(C * G, COLS))


def layer(spread, base, cot, zi, zf, o_buf, g_buf, rows):
    pre, slope_of = {}, {}
    for s in range(NG + 2):
        if s < NG:
            pre[s] = dot(spread[:, rows_of(s), :].reshape(C * G, 4 * K), zi[...]) + base[s]
        if 1 <= s <= NG:
            at = rows_of(s - 1)
            value, slope = gelu_terms(pre.pop(s - 1))
            o_buf[:, at, :] = value.astype(BF).reshape(C, G, COLS)
            gp = (cot[:, at, :].reshape(C * G, COLS).astype(F32) * slope).astype(BF)
            g_buf[:, at, :] = gp.reshape(C, G, COLS)
            slope_of[s - 1] = gp
        if s >= 2:
            r = dot(slope_of.pop(s - 2), zf[...]).astype(BF)
            rows[:, rows_of(s - 2), :] = r.reshape(C, G, 4 * K)


def input_gradient(modes, base, zi, yi, wide, spread, out):
    inverse_y(modes, yi, wide, spread)
    for g in range(NG):
        at = rows_of(g)
        v = dot(spread[:, at, :].reshape(C * G, 4 * K), zi[...]) + base[g]
        out[:, at, :] = v.astype(BF).reshape(C, G, COLS)


def point_gradient(g_buf, f_buf, acc, bias_acc, first):
    total, sums = 0.0, 0.0
    for q in range(0, NG, 4):
        gs = [g_buf[:, rows_of(q + e), :].reshape(C * G, COLS) for e in range(4)]
        fs = [f_buf[:, rows_of(q + e), :].reshape(C * G, COLS) for e in range(4)]
        total = total + dot_nt(jnp.concatenate(gs, axis=1), jnp.concatenate(fs, axis=1))
        for gp in gs:
            gp = gp.astype(F32)
            sums = sums + gp[:, : COLS // 2] + gp[:, COLS // 2 :]
    acc[...] = total if first else acc[...] + total
    bias_acc[...] = sums if first else bias_acc[...] + sums


def main_kernel(
    field, cot, weights, zf_all, zi_all, yf_all, yi_all, point, bias, over_o_ref, over_i_ref,
    out, first, base1, modes_out, grad, zi, yi, small_out,
    f_buf, c_buf, spread, rows, g_buf, base0, wide, part, modes, part2, modes2,
    zf, yf, kron, kron_back, bias_col, acc, bias_acc, w_all, spec, dual, s_small, r_small,
    b1, b2, sems, w_sems, small_sems,
):
    at = places()
    gy, gz = lax.axis_index("gy"), lax.axis_index("gz")
    local = pltpu.make_async_copy
    half = C // 2
    loads = [
        local(field.at[:half, 0], f_buf.at[0, :half], sems.at[0]),
        local(zf_all.at[gz], zf, sems.at[1]),
        local(field.at[half:, 0], f_buf.at[0, half:], sems.at[2]),
        local(yf_all.at[gy], yf, sems.at[3]),
        local(field.at[:, 1], f_buf.at[1], sems.at[4]),
        local(weights, w_all.at[at["hi"]], sems.at[5]),
        local(zi_all.at[gz], zi, sems.at[6]),
        local(yi_all.at[gy], yi, sems.at[7]),
        local(cot.at[:, 0], c_buf.at[0], sems.at[8]),
        local(cot.at[:, 1], c_buf.at[1], sems.at[9]),
    ]
    barrier, partners = greet(at)
    for load in loads[:5]:
        load.start()

    loads[0].wait()
    loads[1].wait()
    forward_z(f_buf.at[0], zf, rows.at[0], 0, half)
    loads[2].wait()
    forward_z(f_buf.at[0], zf, rows.at[0], half, C)
    loads[3].wait()
    forward_y(rows.at[0], yf, wide.at[0], part.at[0])
    pl.semaphore_wait(barrier, partners)
    f0 = scatter_core(at, 0, part, b1)
    w_there = pltpu.make_async_remote_copy(
        src_ref=weights,
        dst_ref=w_all.at[at["hi"]],
        send_sem=w_sems.at[0],
        recv_sem=w_sems.at[1],
        device_id=device(at, hi=1 - at["hi"]),
        device_id_type=MESH,
    )
    loads[4].wait()
    forward_z(f_buf.at[1], zf, rows.at[1], 0, C)
    arrived(f0)
    f0 = scatter_rows(at, 0, part, b1)
    forward_y(rows.at[1], yf, wide.at[1], part.at[1])
    f1 = scatter_core(at, 1, part, b1)
    same, over = group_masks()
    kron[...] = kron_of(dot(over, point[...]), over, same)
    bias_wide = jnp.broadcast_to(bias[...].astype(F32), (2 * K, C)).astype(BF)
    bias_col[...] = dot_nt(over, bias_wide)
    over_o, over_i = over_o_ref[...], over_i_ref[...]
    arrived(f1)
    f1 = scatter_rows(at, 1, part, b1)
    w_there.start()
    for load in loads[5:8]:
        load.start()
    pointwise(f_buf.at[0], kron, bias_col, base0)
    arrived(f0)
    f0 = scatter_halves(at, 0, b1)
    for load in loads[8:]:
        load.start()
    pointwise(f_buf.at[1], kron, bias_col, base1)
    for load in loads[5:8]:
        load.wait()
    w_there.wait()
    w = w_all[...].reshape(K, 2 * C * C)
    arrived(f0)
    mix(at, 0, scatter_total(at, 0, b1), w, over_o, over_i, modes, spec)
    f0 = gather_rows(at, 0, modes, b1)
    arrived(f1)
    f1 = scatter_halves(at, 1, b1)
    kron_back[...] = kron_of(dot_nt(over, point[...]), over, same)
    arrived(f1)
    mix(at, 1, scatter_total(at, 1, b1), w, over_o, over_i, modes, spec)
    f1 = gather_rows(at, 1, modes, b1)
    f0 = gather_core(at, 0, modes, b1, f0)

    for load in loads[8:]:
        load.wait()
    arrived(f0)
    inverse_y(modes.at[0], yi, wide.at[0], spread.at[0])
    layer(spread.at[0], base0, c_buf.at[0], zi, zf, out.at[0], g_buf.at[0], rows.at[0])
    f1 = gather_core(at, 1, modes, b1, f1)
    forward_y(rows.at[0], yf, wide.at[0], part2.at[0])
    f0 = scatter_core(at, 0, part2, b2)
    arrived(f1)
    inverse_y(modes.at[1], yi, wide.at[1], spread.at[1])
    arrived(f0)
    f0 = scatter_rows(at, 0, part2, b2)
    layer(spread.at[1], base1, c_buf.at[1], zi, zf, out.at[1], g_buf.at[1], rows.at[1])
    forward_y(rows.at[1], yf, wide.at[1], part2.at[1])
    f1 = scatter_core(at, 1, part2, b2)

    point_gradient(g_buf.at[0], f_buf.at[0], acc, bias_acc, True)
    arrived(f1)
    f1 = scatter_rows(at, 1, part2, b2)
    arrived(f0)
    f0 = scatter_halves(at, 0, b2)
    point_gradient(g_buf.at[1], f_buf.at[1], acc, bias_acc, False)
    same, over = group_masks()
    kept = jnp.where(same, acc[...], 0.0).reshape(C, G, C * G).sum(axis=1)
    term = jnp.dot(kept, over.astype(F32), precision=lax.Precision.HIGHEST)
    total = bias_acc[...].reshape(C, G, COLS // 2).sum(axis=1).sum(axis=1, keepdims=True)
    s_small[0, :8] = fold(term)
    s_small[0, 8:] = fold(jnp.broadcast_to(total, (C, C)))
    small = [
        send(s_small.at[0], r_small.at[n], small_sems, n, to) for n, to in enumerate(across(at))
    ]
    arrived(f0)
    unmix(at, 0, scatter_total(at, 0, b2), w, over_o, over_i, modes2, dual)
    f0 = gather_rows(at, 0, modes2, b2)
    arrived(f1)
    f1 = scatter_halves(at, 1, b2)
    pointwise_back(g_buf.at[0], kron_back, base0)
    pointwise_back(g_buf.at[1], kron_back, base1)
    arrived(small)
    s_small[1] = s_small[0] + r_small[0] + r_small[1] + r_small[2]
    arrived(f1)
    unmix(at, 1, scatter_total(at, 1, b2), w, over_o, over_i, modes2, dual)
    f1 = gather_rows(at, 1, modes2, b2)
    small = [
        send(s_small.at[1], r_small.at[3 + n], small_sems, 3 + n, device(at, **moved(at, step)))
        for n, step in enumerate(STEPS)
    ]
    weight_gradient(at, spec, dual, over_o, over_i, grad)
    f0 = gather_core(at, 0, modes2, b2, f0)
    arrived(f0)
    input_gradient(modes2.at[0], base0, zi, yi, wide.at[0], spread.at[0], first)
    f1 = gather_core(at, 1, modes2, b2, f1)
    arrived(small)
    total = s_small[1]
    for n in range(len(STEPS)):
        total = total + r_small[3 + n]
    small_out[...] = total * (1.0 / math.sqrt(X * Y * Z))
    arrived(f1)
    modes_out[...] = modes2[1]


def last_kernel(
    held, first, base, modes, grad_in, zi, yi, small,
    out, output, grad, term, total, spread, second, wide, out_sems,
):
    local = pltpu.make_async_copy
    outs = [
        local(first, out.at[:, 0], out_sems.at[0]),
        local(held.at[0], output.at[:, 0], out_sems.at[1]),
        local(held.at[1], output.at[:, 1], out_sems.at[2]),
        local(grad_in, grad, out_sems.at[3]),
    ]
    for copy in outs:
        copy.start()
    term[...] = unfold(small[:8])
    total[...] = unfold(small[8:]).T[:1]
    input_gradient(modes, base, zi, yi, wide, spread, second)
    outs.append(local(second, out.at[:, 1], out_sems.at[4]))
    outs[-1].start()
    for copy in outs:
        copy.wait()


VMEM = pl.BlockSpec(memory_space=pltpu.VMEM)
ANY = pl.BlockSpec(memory_space=pl.ANY)


def params(mib, collective_id=None):
    limit = mib * 1024 * 1024
    if collective_id is None:
        return pltpu.CompilerParams(vmem_limit_bytes=limit)
    return pltpu.CompilerParams(
        vmem_limit_bytes=limit, collective_id=collective_id, has_side_effects=True
    )


def grid_buffer(dtype=BF):
    return pltpu.VMEM((X, C, ROWS, COLS), dtype)


def local(field, spec_weight, point_weight, bias, cotangent):
    zf, zi, yf, yi = (jnp.asarray(t) for t in make_tables())
    over_o, over_i = (jnp.asarray(t) for t in make_spreads())
    shape = jax.ShapeDtypeStruct
    deep = (X, 2, 4, 4, 2, C, 2 * K)
    lines = pltpu.VMEM((X, C, ROWS, 4 * K), BF)
    sample = pltpu.VMEM((C, ROWS, COLS), BF)
    rows_wide = pltpu.VMEM((NG, C * G, COLS), F32)
    wide = (K * C, 2 * K)
    table = pltpu.VMEM((COLS, COLS), BF)
    vmem = pltpu.VMEM
    dma = pltpu.SemaphoreType.DMA
    square = (C * G, C * G)

    held, first, base, modes, grad_spec, zi, yi, small = pl.pallas_call(
        main_kernel,
        out_shape=(
            grid_buffer(),
            sample,
            rows_wide,
            vmem(deep[1:], BF),
            vmem((K // 2, 2 * C * C), F32),
            table,
            vmem((2 * ROWS, K), BF),
            vmem((16, 4 * C), F32),
        ),
        in_specs=[ANY] * 7 + [VMEM] * 4,
        out_specs=[VMEM] * 8,
        scratch_shapes=[
            grid_buffer(), grid_buffer(), lines, lines, grid_buffer(), rows_wide,
            vmem((X,) + wide, F32), vmem(deep, BF), vmem(deep, BF), vmem(deep, BF), vmem(deep, BF),
            table, vmem((K, 2 * ROWS), BF),
            vmem(square, BF), vmem(square, BF), vmem((C * G, 2 * K), F32), vmem(square, F32),
            vmem((C * G, COLS // 2), F32),
            vmem((2, K // 2, 2 * C * C), BF),
            vmem((X, 2 * K, C), F32), vmem((X, 2 * K, C), F32),
            vmem((2, 16, 4 * C), F32), vmem((3 + len(STEPS), 16, 4 * C), F32),
            exchange_scratch(), exchange_scratch(),
            dma((10,)), dma((2,)), [dma((3 + len(STEPS),)), dma((3 + len(STEPS),))],
        ],
        compiler_params=params(51, 1),
        name="layer",
    )(
        field, cotangent, spec_weight, zf, zi, yf, yi,
        point_weight, bias.reshape(1, C), over_o, over_i,
    )

    grad_input, output, grad, term, total = pl.pallas_call(
        last_kernel,
        out_shape=(
            shape(field.shape, BF),
            shape(field.shape, BF),
            shape(grad_spec.shape, F32),
            shape((C, C), F32),
            shape((1, C), F32),
        ),
        in_specs=[VMEM] * 8,
        out_specs=[ANY] * 3 + [VMEM] * 2,
        scratch_shapes=[vmem((C, ROWS, 4 * K), BF), sample, vmem(wide, F32), dma((5,))],
        compiler_params=params(24),
        name="input_gradient",
    )(held, first, base, modes, grad_spec, zi, yi, small)

    return output, grad_input, grad, term, total.reshape(C)


def solution(mesh):
    grid = P(None, None, "gy", "gz")
    owned = P(("gy", "gz"), None)
    return jax.shard_map(
        local,
        mesh=mesh,
        in_specs=(grid, owned, P(), P(), grid),
        out_specs=(grid, grid, owned, P(), P()),
        check_vma=False,
    )
```

```python
import functools
import math

import jax
import jax.numpy as jnp
import numpy as np
from jax import lax
from jax.experimental import pallas as pl
from jax.experimental.pallas import tpu as pltpu

P = jax.sharding.PartitionSpec
BF = jnp.bfloat16
F32 = jnp.float32

C = 32
X = 2
Y = 2048
Z = 2048
K = 64
ROWS = 128
COLS = 256
G = 16
NG = ROWS // G

MESH = pl.DeviceIdType.MESH


def row_order():
    order = []
    for core in range(2):
        for cx in range(4):
            for cy in range(4):
                for lo in range(2):
                    order.append(cx * 16 + lo * 8 + core * 4 + cy)
    return np.array(order)


def make_tables():
    j = row_order()
    fy = np.where(j < K // 2, j, Y - K + j)
    y = np.arange(Y)
    ang_y = 2.0 * np.pi * ((fy[:, None] * y[None, :]) % Y) / Y
    z = np.arange(Z)
    ang_z = 2.0 * np.pi * ((np.arange(K)[:, None] * z[None, :]) % Z) / Z
    cy, sy = np.cos(ang_y), np.sin(ang_y)
    cz, sz = np.cos(ang_z), np.sin(ang_z)
    zf = np.concatenate([cz, -sz, -sz, -cz], axis=0)
    zf = zf.reshape(4 * K, Z // COLS, COLS).transpose(1, 0, 2)
    yf = np.stack([cy, sy], axis=0).reshape(2, K, Y // ROWS, ROWS)
    yf = yf.transpose(2, 1, 0, 3).reshape(Y // ROWS, K, 2 * ROWS)
    yi = np.stack([cy, sy], axis=0).reshape(2, K, Y // ROWS, ROWS)
    yi = yi.transpose(2, 0, 3, 1).reshape(Y // ROWS, 2 * ROWS, K)
    bf = lambda a: np.ascontiguousarray(a).astype(jnp.bfloat16)
    scale = 1.0 / math.sqrt(Y * Z)
    return (
        bf(zf.transpose(0, 2, 1)),
        bf(zf),
        bf(yf * scale),
        bf(yi * (2.0 * scale)),
    )


def make_spreads():
    lane = np.arange(C * C)
    rows = np.arange(C)[:, None]
    over_o = (lane[None, :] // C == rows).astype(np.float32)
    over_i = (lane[None, :] % C == rows).astype(np.float32)
    return over_o.astype(jnp.bfloat16), over_i.astype(jnp.bfloat16)


def dot(a, b):
    return jnp.dot(a, b, preferred_element_type=F32)


def dot_nt(a, b):
    return lax.dot_general(a, b, (((1,), (1,)), ((), ())), preferred_element_type=F32)


def split(v):
    hi = v.astype(BF)
    return hi, (v - hi.astype(F32)).astype(BF)


def forward_z(src, zf, rows, begin, end):
    for c in range(begin, end, 4):
        f = src[pl.ds(c, 4)].reshape(4 * ROWS, COLS)
        rows[pl.ds(c, 4)] = dot(f, zf[...]).astype(BF).reshape(4, ROWS, 4 * K)


def forward_y(rows, yf, wide, part):
    for c in range(0, C, 2):
        one, two = rows[c], rows[c + 1]
        upper = jnp.concatenate([one[:, : 2 * K], two[:, : 2 * K]], axis=1)
        lower = jnp.concatenate([one[:, 2 * K :], two[:, 2 * K :]], axis=1)
        r = dot(yf[...], jnp.concatenate([upper, lower], axis=0))
        wide[pl.ds(c, K, stride=C), :] = r[:, : 2 * K]
        wide[pl.ds(c + 1, K, stride=C), :] = r[:, 2 * K :]
    step = K * C // 8
    for n in range(8):
        part[n // 4, n % 4] = wide[pl.ds(n * step, step), :].astype(BF).reshape(4, 2, C, 2 * K)


def inverse_y(modes, yi, wide, spread):
    step = K * C // 8
    for n in range(8):
        wide[pl.ds(n * step, step), :] = modes[n // 4, n % 4].astype(F32).reshape(step, 2 * K)
    for c in range(0, C, 2):
        one = wide[pl.ds(c, K, stride=C), :].astype(BF)
        two = wide[pl.ds(c + 1, K, stride=C), :].astype(BF)
        r = dot(yi[...], jnp.concatenate([one, two], axis=1)).astype(BF)
        for e in range(2):
            lanes = slice(e * 2 * K, (e + 1) * 2 * K)
            spread[c + e, :, : 2 * K] = r[:ROWS, lanes]
            spread[c + e, :, 2 * K :] = r[ROWS:, lanes]


def fold(v):
    return jnp.concatenate([v[8 * n : 8 * n + 8] for n in range(C // 8)], axis=1)


def unfold(v):
    return jnp.concatenate([v[:, C * n : C * n + C] for n in range(C // 8)], axis=0)


def rows_of(g):
    return pl.ds(g * G, G)


def places():
    gy, gz = lax.axis_index("gy"), lax.axis_index("gz")
    return dict(x=gy // 4, lo=gy // 2 % 2, core=gy % 2, y=gz // 2, hi=gz % 2)


def device(at, **other):
    at = dict(at, **other)
    return {
        "gy": at["x"] * 4 + at["lo"] * 2 + at["core"],
        "gz": at["y"] * 2 + at["hi"],
    }


def turned(at, axis, step):
    return lax.rem(at[axis] + step, 4)


STEPS = [(dx, dy, dl) for dx in (2, 1, 3, 0) for dy in (2, 1, 3, 0) for dl in (1, 0)][:-1]


def moved(at, step):
    dx, dy, dl = step
    lo = 1 - at["lo"] if dl else at["lo"]
    return dict(x=turned(at, "x", dx), y=turned(at, "y", dy), lo=lo)


def across(at):
    core, hi = 1 - at["core"], 1 - at["hi"]
    return [device(at, core=core), device(at, hi=hi), device(at, core=core, hi=hi)]


def greet(at):
    barrier = pltpu.get_barrier_semaphore()
    partners = across(at) + [device(at, **moved(at, step)) for step in STEPS]
    for partner in partners:
        pl.semaphore_signal(barrier, inc=1, device_id=partner, device_id_type=MESH)
    return barrier, len(partners)


def send(src, dst, sems, n, to):
    send_sem, recv_sem = sems
    copy = pltpu.make_async_remote_copy(
        src_ref=src,
        dst_ref=dst,
        send_sem=send_sem.at[n],
        recv_sem=recv_sem.at[n],
        device_id=to,
        device_id_type=MESH,
    )
    copy.start()
    return copy


def arrived(copies):
    for copy in copies:
        copy.wait()


def scatter_core(at, p, part, b):
    other = 1 - at["core"]
    return [send(part.at[p, other], b["r1"].at[p], b["core_in"], p, device(at, core=other))]


def scatter_rows(at, p, part, b):
    me = at["core"]
    copies = []
    for dx in (2, 1, 3, 0):
        cx = turned(at, "x", dx)
        b["s1"][p, cx] = (part[p, me, cx].astype(F32) + b["r1"][p, cx].astype(F32)).astype(BF)
        for n, step in enumerate(STEPS):
            if step[0] == dx:
                to = moved(at, step)
                copies.append(
                    send(
                        b["s1"].at[p, cx, to["y"], to["lo"]],
                        b["r2"].at[p, n],
                        b["rows_in"],
                        p * len(STEPS) + n,
                        device(at, **to),
                    )
                )
    return copies


def scatter_halves(at, p, b):
    total = b["s1"][p, at["x"], at["y"], at["lo"]].astype(F32)
    for n in range(len(STEPS)):
        total = total + b["r2"][p, n].astype(F32)
    b["s3"][p] = total
    return [send(b["s3"].at[p], b["r4"].at[p], b["half_in"], p, device(at, hi=1 - at["hi"]))]


def scatter_total(at, p, b):
    return b["s3"][p] + b["r4"][p]


def gather_rows(at, p, modes, b):
    here = modes.at[p, at["core"], at["x"], at["y"], at["lo"]]
    return [
        send(here, here, b["rows_out"], p * len(STEPS) + n, device(at, **moved(at, step)))
        for n, step in enumerate(STEPS)
    ]


def gather_core(at, p, modes, b, copies):
    passed = []
    for dx in (0, 1, 3, 2):
        arrived([copy for copy, step in zip(copies, STEPS) if step[0] == dx])
        block = modes.at[p, at["core"], turned(at, "x", 4 - dx)]
        passed.append(send(block, block, b["core_out"], 4 * p + dx, device(at, core=1 - at["core"])))
    return passed


def exchange_scratch():
    pair = lambda n: [pltpu.SemaphoreType.DMA((n,)), pltpu.SemaphoreType.DMA((n,))]
    rows = len(STEPS)
    return dict(
        r1=pltpu.VMEM((X, 4, 4, 2, C, 2 * K), BF),
        s1=pltpu.VMEM((X, 4, 4, 2, C, 2 * K), BF),
        r2=pltpu.VMEM((X, rows, C, 2 * K), BF),
        s3=pltpu.VMEM((X, C, 2 * K), F32),
        r4=pltpu.VMEM((X, C, 2 * K), F32),
        core_in=pair(X),
        rows_in=pair(X * rows),
        half_in=pair(X),
        rows_out=pair(X * rows),
        core_out=pair(4 * X),
    )


def widen(v, table):
    hi, lo = split(v)
    return dot(hi, table) + dot(lo, table)


def narrow(v, table):
    hi, lo = split(v)
    return dot_nt(hi, table) + dot_nt(lo, table)


def put_modes(at, p, modes, real, imag):
    block = jnp.concatenate([real, imag], axis=0).T
    modes[p, at["core"], at["x"], at["y"], at["lo"]] = block.astype(BF)


def mix(at, p, total, w_all, over_o, over_i, modes, spec):
    t = total.T
    spec[p] = t
    s_real = widen(t[:K], over_o)
    s_imag = widen(t[K:], over_o)
    w_real, w_imag = w_all[:, : C * C].astype(F32), w_all[:, C * C :].astype(F32)
    real = narrow(w_real * s_real - w_imag * s_imag, over_i)
    imag = narrow(w_real * s_imag + w_imag * s_real, over_i)
    put_modes(at, p, modes, real, imag)


def unmix(at, p, total, w_all, over_o, over_i, modes, dual):
    t = total.T * 2.0
    dual[p] = t
    d_real = widen(t[:K], over_i)
    d_imag = widen(t[K:], over_i)
    w_real, w_imag = w_all[:, : C * C].astype(F32), w_all[:, C * C :].astype(F32)
    real = narrow(w_real * d_real + w_imag * d_imag, over_o)
    imag = narrow(w_real * d_imag - w_imag * d_real, over_o)
    put_modes(at, p, modes, real * 0.5, imag * 0.5)


def weight_gradient(at, spec, dual, over_o, over_i, grad):
    half = K // 2
    real, imag = 0.0, 0.0
    for p in range(X):
        top = pl.ds(pl.multiple_of(at["hi"] * half, half), half)
        low = pl.ds(pl.multiple_of(at["hi"] * half + K, half), half)
        s_real, s_imag = widen(spec[p, top], over_o), widen(spec[p, low], over_o)
        d_real, d_imag = widen(dual[p, top], over_i), widen(dual[p, low], over_i)
        real = real + d_real * s_real + d_imag * s_imag
        imag = imag + d_imag * s_real - d_real * s_imag
    grad[:, : C * C] = real
    grad[:, C * C :] = imag


def gelu_terms(v):
    phi = 0.5 + 0.5 * lax.erf(v * math.sqrt(0.5))
    return v * phi, phi + v * jnp.exp(v * v * -0.5) * (1.0 / math.sqrt(2.0 * math.pi))


def group_masks():
    a = lax.broadcasted_iota(jnp.int32, (C * G, C * G), 0)
    b = lax.broadcasted_iota(jnp.int32, (C * G, C * G), 1)
    same = ((a ^ b) & (G - 1)) == 0
    m = lax.broadcasted_iota(jnp.int32, (C * G, C), 0)
    n = lax.broadcasted_iota(jnp.int32, (C * G, C), 1)
    over = (m - n * G).astype(F32)
    over = jnp.where((over >= 0.0) & (over < float(G)), 1.0, 0.0).astype(BF)
    return same, over


def kron_of(half, over, same):
    return jnp.where(same, dot_nt(half.astype(BF), over), 0.0).astype(BF)


def pointwise(f_buf, kron, bias_col, base):
    for g in range(NG):
        f = f_buf[:, rows_of(g), :].reshape(C * G, COLS)
        base[g] = dot(kron[...], f) + bias_col[:, :1]


def pointwise_back(g_buf, kron, base):
    for g in range(NG):
        base[g] = dot(kron[...], g_buf[:, rows_of(g), :].reshape(C * G, COLS))


def layer(spread, base, cot, zi, zf, o_buf, g_buf, rows):
    pre, slope_of = {}, {}
    for s in range(NG + 2):
        if s < NG:
            pre[s] = dot(spread[:, rows_of(s), :].reshape(C * G, 4 * K), zi[...]) + base[s]
        if 1 <= s <= NG:
            at = rows_of(s - 1)
            value, slope = gelu_terms(pre.pop(s - 1))
            o_buf[:, at, :] = value.astype(BF).reshape(C, G, COLS)
            gp = (cot[:, at, :].reshape(C * G, COLS).astype(F32) * slope).astype(BF)
            g_buf[:, at, :] = gp.reshape(C, G, COLS)
            slope_of[s - 1] = gp
        if s >= 2:
            r = dot(slope_of.pop(s - 2), zf[...]).astype(BF)
            rows[:, rows_of(s - 2), :] = r.reshape(C, G, 4 * K)


def input_gradient(modes, base, zi, yi, wide, spread, out):
    inverse_y(modes, yi, wide, spread)
    for g in range(NG):
        at = rows_of(g)
        v = dot(spread[:, at, :].reshape(C * G, 4 * K), zi[...]) + base[g]
        out[:, at, :] = v.astype(BF).reshape(C, G, COLS)


def point_gradient(g_buf, f_buf, acc, bias_acc, first):
    total, sums = 0.0, 0.0
    for q in range(0, NG, 4):
        gs = [g_buf[:, rows_of(q + e), :].reshape(C * G, COLS) for e in range(4)]
        fs = [f_buf[:, rows_of(q + e), :].reshape(C * G, COLS) for e in range(4)]
        total = total + dot_nt(jnp.concatenate(gs, axis=1), jnp.concatenate(fs, axis=1))
        for gp in gs:
            gp = gp.astype(F32)
            sums = sums + gp[:, : COLS // 2] + gp[:, COLS // 2 :]
    acc[...] = total if first else acc[...] + total
    bias_acc[...] = sums if first else bias_acc[...] + sums


def main_kernel(
    field, cot, weights, zf_all, zi_all, yf_all, yi_all, point, bias, over_o_ref, over_i_ref,
    out, first, base1, modes_out, grad, zi, yi, small_out,
    f_buf, c_buf, spread, rows, g_buf, base0, wide, part, modes, part2, modes2,
    zf, yf, kron, kron_back, bias_col, acc, bias_acc, w_all, spec, dual, s_small, r_small,
    b1, b2, sems, w_sems, small_sems,
):
    at = places()
    gy, gz = lax.axis_index("gy"), lax.axis_index("gz")
    local = pltpu.make_async_copy
    half = C // 2
    loads = [
        local(field.at[:half, 0], f_buf.at[0, :half], sems.at[0]),
        local(zf_all.at[gz], zf, sems.at[1]),
        local(field.at[half:, 0], f_buf.at[0, half:], sems.at[2]),
        local(yf_all.at[gy], yf, sems.at[3]),
        local(field.at[:, 1], f_buf.at[1], sems.at[4]),
        local(weights, w_all.at[at["hi"]], sems.at[5]),
        local(zi_all.at[gz], zi, sems.at[6]),
        local(yi_all.at[gy], yi, sems.at[7]),
        local(cot.at[:, 0], c_buf.at[0], sems.at[8]),
        local(cot.at[:, 1], c_buf.at[1], sems.at[9]),
    ]
    barrier, partners = greet(at)
    for load in loads[:5]:
        load.start()

    loads[0].wait()
    loads[1].wait()
    forward_z(f_buf.at[0], zf, rows.at[0], 0, half)
    loads[2].wait()
    forward_z(f_buf.at[0], zf, rows.at[0], half, C)
    loads[3].wait()
    forward_y(rows.at[0], yf, wide.at[0], part.at[0])
    pl.semaphore_wait(barrier, partners)
    f0 = scatter_core(at, 0, part, b1)
    w_there = pltpu.make_async_remote_copy(
        src_ref=weights,
        dst_ref=w_all.at[at["hi"]],
        send_sem=w_sems.at[0],
        recv_sem=w_sems.at[1],
        device_id=device(at, hi=1 - at["hi"]),
        device_id_type=MESH,
    )
    loads[4].wait()
    forward_z(f_buf.at[1], zf, rows.at[1], 0, C)
    arrived(f0)
    f0 = scatter_rows(at, 0, part, b1)
    forward_y(rows.at[1], yf, wide.at[1], part.at[1])
    f1 = scatter_core(at, 1, part, b1)
    same, over = group_masks()
    kron[...] = kron_of(dot(over, point[...]), over, same)
    bias_wide = jnp.broadcast_to(bias[...].astype(F32), (2 * K, C)).astype(BF)
    bias_col[...] = dot_nt(over, bias_wide)
    over_o, over_i = over_o_ref[...], over_i_ref[...]
    w_there.start()
    for load in loads[5:8]:
        load.start()
    pointwise(f_buf.at[0], kron, bias_col, base0)
    arrived(f0)
    f0 = scatter_halves(at, 0, b1)
    arrived(f1)
    f1 = scatter_rows(at, 1, part, b1)
    for load in loads[8:]:
        load.start()
    pointwise(f_buf.at[1], kron, bias_col, base1)
    for load in loads[5:8]:
        load.wait()
    w_there.wait()
    w = w_all[...].reshape(K, 2 * C * C)
    arrived(f0)
    mix(at, 0, scatter_total(at, 0, b1), w, over_o, over_i, modes, spec)
    f0 = gather_rows(at, 0, modes, b1)
    arrived(f1)
    f1 = scatter_halves(at, 1, b1)
    kron_back[...] = kron_of(dot_nt(over, point[...]), over, same)
    arrived(f1)
    mix(at, 1, scatter_total(at, 1, b1), w, over_o, over_i, modes, spec)
    f1 = gather_rows(at, 1, modes, b1)
    f0 = gather_core(at, 0, modes, b1, f0)

    for load in loads[8:]:
        load.wait()
    arrived(f0)
    inverse_y(modes.at[0], yi, wide.at[0], spread.at[0])
    layer(spread.at[0], base0, c_buf.at[0], zi, zf, out.at[0], g_buf.at[0], rows.at[0])
    f1 = gather_core(at, 1, modes, b1, f1)
    forward_y(rows.at[0], yf, wide.at[0], part2.at[0])
    f0 = scatter_core(at, 0, part2, b2)
    arrived(f1)
    inverse_y(modes.at[1], yi, wide.at[1], spread.at[1])
    arrived(f0)
    f0 = scatter_rows(at, 0, part2, b2)
    layer(spread.at[1], base1, c_buf.at[1], zi, zf, out.at[1], g_buf.at[1], rows.at[1])
    forward_y(rows.at[1], yf, wide.at[1], part2.at[1])
    f1 = scatter_core(at, 1, part2, b2)

    point_gradient(g_buf.at[0], f_buf.at[0], acc, bias_acc, True)
    arrived(f1)
    f1 = scatter_rows(at, 1, part2, b2)
    arrived(f0)
    f0 = scatter_halves(at, 0, b2)
    point_gradient(g_buf.at[1], f_buf.at[1], acc, bias_acc, False)
    same, over = group_masks()
    kept = jnp.where(same, acc[...], 0.0).reshape(C, G, C * G).sum(axis=1)
    term = jnp.dot(kept, over.astype(F32), precision=lax.Precision.HIGHEST)
    total = bias_acc[...].reshape(C, G, COLS // 2).sum(axis=1).sum(axis=1, keepdims=True)
    s_small[0, :8] = fold(term)
    s_small[0, 8:] = fold(jnp.broadcast_to(total, (C, C)))
    small = [
        send(s_small.at[0], r_small.at[n], small_sems, n, to) for n, to in enumerate(across(at))
    ]
    arrived(f0)
    unmix(at, 0, scatter_total(at, 0, b2), w, over_o, over_i, modes2, dual)
    arrived(f1)
    f1 = scatter_halves(at, 1, b2)
    f0 = gather_rows(at, 0, modes2, b2)
    pointwise_back(g_buf.at[0], kron_back, base0)
    pointwise_back(g_buf.at[1], kron_back, base1)
    arrived(small)
    s_small[1] = s_small[0] + r_small[0] + r_small[1] + r_small[2]
    arrived(f1)
    unmix(at, 1, scatter_total(at, 1, b2), w, over_o, over_i, modes2, dual)
    f1 = gather_rows(at, 1, modes2, b2)
    small = [
        send(s_small.at[1], r_small.at[3 + n], small_sems, 3 + n, device(at, **moved(at, step)))
        for n, step in enumerate(STEPS)
    ]
    weight_gradient(at, spec, dual, over_o, over_i, grad)
    f0 = gather_core(at, 0, modes2, b2, f0)
    arrived(f0)
    input_gradient(modes2.at[0], base0, zi, yi, wide.at[0], spread.at[0], first)
    f1 = gather_core(at, 1, modes2, b2, f1)
    arrived(small)
    total = s_small[1]
    for n in range(len(STEPS)):
        total = total + r_small[3 + n]
    small_out[...] = total * (1.0 / math.sqrt(X * Y * Z))
    arrived(f1)
    modes_out[...] = modes2[1]


def last_kernel(
    held, first, base, modes, grad_in, zi, yi, small,
    out, output, grad, term, total, spread, second, wide, out_sems,
):
    local = pltpu.make_async_copy
    outs = [
        local(first, out.at[:, 0], out_sems.at[0]),
        local(held.at[0], output.at[:, 0], out_sems.at[1]),
        local(held.at[1], output.at[:, 1], out_sems.at[2]),
        local(grad_in, grad, out_sems.at[3]),
    ]
    for copy in outs:
        copy.start()
    term[...] = unfold(small[:8])
    total[...] = unfold(small[8:]).T[:1]
    input_gradient(modes, base, zi, yi, wide, spread, second)
    outs.append(local(second, out.at[:, 1], out_sems.at[4]))
    outs[-1].start()
    for copy in outs:
        copy.wait()


VMEM = pl.BlockSpec(memory_space=pltpu.VMEM)
ANY = pl.BlockSpec(memory_space=pl.ANY)


def params(mib, collective_id=None):
    limit = mib * 1024 * 1024
    if collective_id is None:
        return pltpu.CompilerParams(vmem_limit_bytes=limit)
    return pltpu.CompilerParams(
        vmem_limit_bytes=limit, collective_id=collective_id, has_side_effects=True
    )


def grid_buffer(dtype=BF):
    return pltpu.VMEM((X, C, ROWS, COLS), dtype)


def local(field, spec_weight, point_weight, bias, cotangent):
    zf, zi, yf, yi = (jnp.asarray(t) for t in make_tables())
    over_o, over_i = (jnp.asarray(t) for t in make_spreads())
    shape = jax.ShapeDtypeStruct
    deep = (X, 2, 4, 4, 2, C, 2 * K)
    lines = pltpu.VMEM((X, C, ROWS, 4 * K), BF)
    sample = pltpu.VMEM((C, ROWS, COLS), BF)
    rows_wide = pltpu.VMEM((NG, C * G, COLS), F32)
    wide = (K * C, 2 * K)
    table = pltpu.VMEM((COLS, COLS), BF)
    vmem = pltpu.VMEM
    dma = pltpu.SemaphoreType.DMA
    square = (C * G, C * G)

    held, first, base, modes, grad_spec, zi, yi, small = pl.pallas_call(
        main_kernel,
        out_shape=(
            grid_buffer(),
            sample,
            rows_wide,
            vmem(deep[1:], BF),
            vmem((K // 2, 2 * C * C), F32),
            table,
            vmem((2 * ROWS, K), BF),
            vmem((16, 4 * C), F32),
        ),
        in_specs=[ANY] * 7 + [VMEM] * 4,
        out_specs=[VMEM] * 8,
        scratch_shapes=[
            grid_buffer(), grid_buffer(), lines, lines, grid_buffer(), rows_wide,
            vmem((X,) + wide, F32), vmem(deep, BF), vmem(deep, BF), vmem(deep, BF), vmem(deep, BF),
            table, vmem((K, 2 * ROWS), BF),
            vmem(square, BF), vmem(square, BF), vmem((C * G, 2 * K), F32), vmem(square, F32),
            vmem((C * G, COLS // 2), F32),
            vmem((2, K // 2, 2 * C * C), BF),
            vmem((X, 2 * K, C), F32), vmem((X, 2 * K, C), F32),
            vmem((2, 16, 4 * C), F32), vmem((3 + len(STEPS), 16, 4 * C), F32),
            exchange_scratch(), exchange_scratch(),
            dma((10,)), dma((2,)), [dma((3 + len(STEPS),)), dma((3 + len(STEPS),))],
        ],
        compiler_params=params(51, 1),
        name="layer",
    )(
        field, cotangent, spec_weight, zf, zi, yf, yi,
        point_weight, bias.reshape(1, C), over_o, over_i,
    )

    grad_input, output, grad, term, total = pl.pallas_call(
        last_kernel,
        out_shape=(
            shape(field.shape, BF),
            shape(field.shape, BF),
            shape(grad_spec.shape, F32),
            shape((C, C), F32),
            shape((1, C), F32),
        ),
        in_specs=[VMEM] * 8,
        out_specs=[ANY] * 3 + [VMEM] * 2,
        scratch_shapes=[vmem((C, ROWS, 4 * K), BF), sample, vmem(wide, F32), dma((5,))],
        compiler_params=params(24),
        name="input_gradient",
    )(held, first, base, modes, grad_spec, zi, yi, small)

    return output, grad_input, grad, term, total.reshape(C)


def solution(mesh):
    grid = P(None, None, "gy", "gz")
    owned = P(("gy", "gz"), None)
    return jax.shard_map(
        local,
        mesh=mesh,
        in_specs=(grid, owned, P(), P(), grid),
        out_specs=(grid, grid, owned, P(), P()),
        check_vma=False,
    )
```

```python
import functools
import math

import jax
import jax.numpy as jnp
import numpy as np
from jax import lax
from jax.experimental import pallas as pl
from jax.experimental.pallas import tpu as pltpu

P = jax.sharding.PartitionSpec
BF = jnp.bfloat16
F32 = jnp.float32

C = 32
X = 2
Y = 2048
Z = 2048
K = 64
ROWS = 128
COLS = 256
G = 16
NG = ROWS // G

MESH = pl.DeviceIdType.MESH


def row_order():
    order = []
    for core in range(2):
        for cx in range(4):
            for cy in range(4):
                for lo in range(2):
                    order.append(cx * 16 + lo * 8 + core * 4 + cy)
    return np.array(order)


def make_tables():
    j = row_order()
    fy = np.where(j < K // 2, j, Y - K + j)
    y = np.arange(Y)
    ang_y = 2.0 * np.pi * ((fy[:, None] * y[None, :]) % Y) / Y
    z = np.arange(Z)
    ang_z = 2.0 * np.pi * ((np.arange(K)[:, None] * z[None, :]) % Z) / Z
    cy, sy = np.cos(ang_y), np.sin(ang_y)
    cz, sz = np.cos(ang_z), np.sin(ang_z)
    zf = np.concatenate([cz, -sz, -sz, -cz], axis=0)
    zf = zf.reshape(4 * K, Z // COLS, COLS).transpose(1, 0, 2)
    yf = np.stack([cy, sy], axis=0).reshape(2, K, Y // ROWS, ROWS)
    yf = yf.transpose(2, 1, 0, 3).reshape(Y // ROWS, K, 2 * ROWS)
    yi = np.stack([cy, sy], axis=0).reshape(2, K, Y // ROWS, ROWS)
    yi = yi.transpose(2, 0, 3, 1).reshape(Y // ROWS, 2 * ROWS, K)
    bf = lambda a: np.ascontiguousarray(a).astype(jnp.bfloat16)
    scale = 1.0 / math.sqrt(Y * Z)
    return (
        bf(zf.transpose(0, 2, 1)),
        bf(zf),
        bf(yf * scale),
        bf(yi * (2.0 * scale)),
    )


def make_spreads():
    lane = np.arange(C * C)
    rows = np.arange(C)[:, None]
    over_o = (lane[None, :] // C == rows).astype(np.float32)
    over_i = (lane[None, :] % C == rows).astype(np.float32)
    return over_o.astype(jnp.bfloat16), over_i.astype(jnp.bfloat16)


def dot(a, b):
    return jnp.dot(a, b, preferred_element_type=F32)


def dot_nt(a, b):
    return lax.dot_general(a, b, (((1,), (1,)), ((), ())), preferred_element_type=F32)


def split(v):
    hi = v.astype(BF)
    return hi, (v - hi.astype(F32)).astype(BF)


def forward_z(src, zf, rows, begin, end):
    for c in range(begin, end, 4):
        f = src[pl.ds(c, 4)].reshape(4 * ROWS, COLS)
        rows[pl.ds(c, 4)] = dot(f, zf[...]).astype(BF).reshape(4, ROWS, 4 * K)


def forward_y(rows, yf, wide, part):
    for c in range(0, C, 2):
        one, two = rows[c], rows[c + 1]
        upper = jnp.concatenate([one[:, : 2 * K], two[:, : 2 * K]], axis=1)
        lower = jnp.concatenate([one[:, 2 * K :], two[:, 2 * K :]], axis=1)
        r = dot(yf[...], jnp.concatenate([upper, lower], axis=0))
        wide[pl.ds(c, K, stride=C), :] = r[:, : 2 * K]
        wide[pl.ds(c + 1, K, stride=C), :] = r[:, 2 * K :]
    step = K * C // 8
    for n in range(8):
        part[n // 4, n % 4] = wide[pl.ds(n * step, step), :].astype(BF).reshape(4, 2, C, 2 * K)


def inverse_y(modes, yi, wide, spread):
    step = K * C // 8
    for n in range(8):
        wide[pl.ds(n * step, step), :] = modes[n // 4, n % 4].astype(F32).reshape(step, 2 * K)
    for c in range(0, C, 2):
        one = wide[pl.ds(c, K, stride=C), :].astype(BF)
        two = wide[pl.ds(c + 1, K, stride=C), :].astype(BF)
        r = dot(yi[...], jnp.concatenate([one, two], axis=1)).astype(BF)
        for e in range(2):
            lanes = slice(e * 2 * K, (e + 1) * 2 * K)
            spread[c + e, :, : 2 * K] = r[:ROWS, lanes]
            spread[c + e, :, 2 * K :] = r[ROWS:, lanes]


def fold(v):
    return jnp.concatenate([v[8 * n : 8 * n + 8] for n in range(C // 8)], axis=1)


def unfold(v):
    return jnp.concatenate([v[:, C * n : C * n + C] for n in range(C // 8)], axis=0)


def rows_of(g):
    return pl.ds(g * G, G)


def places():
    gy, gz = lax.axis_index("gy"), lax.axis_index("gz")
    return dict(x=gy // 4, lo=gy // 2 % 2, core=gy % 2, y=gz // 2, hi=gz % 2)


def device(at, **other):
    at = dict(at, **other)
    return {
        "gy": at["x"] * 4 + at["lo"] * 2 + at["core"],
        "gz": at["y"] * 2 + at["hi"],
    }


def turned(at, axis, step):
    return lax.rem(at[axis] + step, 4)


STEPS = [(dx, dy, dl) for dx in (2, 1, 3, 0) for dy in (2, 1, 3, 0) for dl in (1, 0)][:-1]


def moved(at, step):
    dx, dy, dl = step
    lo = 1 - at["lo"] if dl else at["lo"]
    return dict(x=turned(at, "x", dx), y=turned(at, "y", dy), lo=lo)


def across(at):
    core, hi = 1 - at["core"], 1 - at["hi"]
    return [device(at, core=core), device(at, hi=hi), device(at, core=core, hi=hi)]


def greet(at):
    barrier = pltpu.get_barrier_semaphore()
    partners = across(at) + [device(at, **moved(at, step)) for step in STEPS]
    for partner in partners:
        pl.semaphore_signal(barrier, inc=1, device_id=partner, device_id_type=MESH)
    return barrier, len(partners)


def send(src, dst, sems, n, to):
    send_sem, recv_sem = sems
    copy = pltpu.make_async_remote_copy(
        src_ref=src,
        dst_ref=dst,
        send_sem=send_sem.at[n],
        recv_sem=recv_sem.at[n],
        device_id=to,
        device_id_type=MESH,
    )
    copy.start()
    return copy


def arrived(copies):
    for copy in copies:
        copy.wait()


def scatter_core(at, p, part, b):
    other = 1 - at["core"]
    return [send(part.at[p, other], b["r1"].at[p], b["core_in"], p, device(at, core=other))]


def scatter_rows(at, p, part, b):
    me = at["core"]
    copies = []
    for dx in (2, 1, 3, 0):
        cx = turned(at, "x", dx)
        b["s1"][p, cx] = (part[p, me, cx].astype(F32) + b["r1"][p, cx].astype(F32)).astype(BF)
        for n, step in enumerate(STEPS):
            if step[0] == dx:
                to = moved(at, step)
                copies.append(
                    send(
                        b["s1"].at[p, cx, to["y"], to["lo"]],
                        b["r2"].at[p, n],
                        b["rows_in"],
                        p * len(STEPS) + n,
                        device(at, **to),
                    )
                )
    return copies


def scatter_halves(at, p, b):
    total = b["s1"][p, at["x"], at["y"], at["lo"]].astype(F32)
    for n in range(len(STEPS)):
        total = total + b["r2"][p, n].astype(F32)
    b["s3"][p] = total
    return [send(b["s3"].at[p], b["r4"].at[p], b["half_in"], p, device(at, hi=1 - at["hi"]))]


def scatter_total(at, p, b):
    return b["s3"][p] + b["r4"][p]


def gather_rows(at, p, modes, b):
    here = modes.at[p, at["core"], at["x"], at["y"], at["lo"]]
    return [
        send(here, here, b["rows_out"], p * len(STEPS) + n, device(at, **moved(at, step)))
        for n, step in enumerate(STEPS)
    ]


def gather_core(at, p, modes, b, copies):
    passed = []
    for dx in (0, 1, 3, 2):
        arrived([copy for copy, step in zip(copies, STEPS) if step[0] == dx])
        block = modes.at[p, at["core"], turned(at, "x", 4 - dx)]
        passed.append(send(block, block, b["core_out"], 4 * p + dx, device(at, core=1 - at["core"])))
    return passed


def exchange_scratch():
    pair = lambda n: [pltpu.SemaphoreType.DMA((n,)), pltpu.SemaphoreType.DMA((n,))]
    rows = len(STEPS)
    return dict(
        r1=pltpu.VMEM((X, 4, 4, 2, C, 2 * K), BF),
        s1=pltpu.VMEM((X, 4, 4, 2, C, 2 * K), BF),
        r2=pltpu.VMEM((X, rows, C, 2 * K), BF),
        s3=pltpu.VMEM((X, C, 2 * K), F32),
        r4=pltpu.VMEM((X, C, 2 * K), F32),
        core_in=pair(X),
        rows_in=pair(X * rows),
        half_in=pair(X),
        rows_out=pair(X * rows),
        core_out=pair(4 * X),
    )


def widen(v, table):
    hi, lo = split(v)
    return dot(hi, table) + dot(lo, table)


def narrow(v, table):
    hi, lo = split(v)
    return dot_nt(hi, table) + dot_nt(lo, table)


def put_modes(at, p, modes, real, imag):
    block = jnp.concatenate([real, imag], axis=0).T
    modes[p, at["core"], at["x"], at["y"], at["lo"]] = block.astype(BF)


def mix(at, p, total, w_all, over_o, over_i, modes, spec):
    t = total.T
    spec[p] = t
    s_real = widen(t[:K], over_o)
    s_imag = widen(t[K:], over_o)
    w_real, w_imag = w_all[:, : C * C].astype(F32), w_all[:, C * C :].astype(F32)
    real = narrow(w_real * s_real - w_imag * s_imag, over_i)
    imag = narrow(w_real * s_imag + w_imag * s_real, over_i)
    put_modes(at, p, modes, real, imag)


def unmix(at, p, total, w_all, over_o, over_i, modes, dual):
    t = total.T * 2.0
    dual[p] = t
    d_real = widen(t[:K], over_i)
    d_imag = widen(t[K:], over_i)
    w_real, w_imag = w_all[:, : C * C].astype(F32), w_all[:, C * C :].astype(F32)
    real = narrow(w_real * d_real + w_imag * d_imag, over_o)
    imag = narrow(w_real * d_imag - w_imag * d_real, over_o)
    put_modes(at, p, modes, real * 0.5, imag * 0.5)


def weight_gradient(at, spec, dual, over_o, over_i, grad):
    half = K // 2
    real, imag = 0.0, 0.0
    for p in range(X):
        top = pl.ds(pl.multiple_of(at["hi"] * half, half), half)
        low = pl.ds(pl.multiple_of(at["hi"] * half + K, half), half)
        s_real, s_imag = widen(spec[p, top], over_o), widen(spec[p, low], over_o)
        d_real, d_imag = widen(dual[p, top], over_i), widen(dual[p, low], over_i)
        real = real + d_real * s_real + d_imag * s_imag
        imag = imag + d_imag * s_real - d_real * s_imag
    grad[:, : C * C] = real
    grad[:, C * C :] = imag


def gelu_terms(v):
    phi = 0.5 + 0.5 * lax.erf(v * math.sqrt(0.5))
    return v * phi, phi + v * jnp.exp(v * v * -0.5) * (1.0 / math.sqrt(2.0 * math.pi))


def group_masks():
    a = lax.broadcasted_iota(jnp.int32, (C * G, C * G), 0)
    b = lax.broadcasted_iota(jnp.int32, (C * G, C * G), 1)
    same = ((a ^ b) & (G - 1)) == 0
    m = lax.broadcasted_iota(jnp.int32, (C * G, C), 0)
    n = lax.broadcasted_iota(jnp.int32, (C * G, C), 1)
    over = (m - n * G).astype(F32)
    over = jnp.where((over >= 0.0) & (over < float(G)), 1.0, 0.0).astype(BF)
    return same, over


def kron_of(half, over, same):
    return jnp.where(same, dot_nt(half.astype(BF), over), 0.0).astype(BF)


def pointwise(f_buf, kron, bias_col, base):
    for g in range(NG):
        f = f_buf[:, rows_of(g), :].reshape(C * G, COLS)
        base[g] = dot(kron[...], f) + bias_col[:, :1]


def pointwise_back(g_buf, kron, base):
    for g in range(NG):
        base[g] = dot(kron[...], g_buf[:, rows_of(g), :].reshape(C * G, COLS))


def layer(spread, base, cot, zi, zf, o_buf, g_buf, rows):
    pre, slope_of = {}, {}
    for s in range(NG + 2):
        if s < NG:
            pre[s] = dot(spread[:, rows_of(s), :].reshape(C * G, 4 * K), zi[...]) + base[s]
        if 1 <= s <= NG:
            at = rows_of(s - 1)
            value, slope = gelu_terms(pre.pop(s - 1))
            o_buf[:, at, :] = value.astype(BF).reshape(C, G, COLS)
            gp = (cot[:, at, :].reshape(C * G, COLS).astype(F32) * slope).astype(BF)
            g_buf[:, at, :] = gp.reshape(C, G, COLS)
            slope_of[s - 1] = gp
        if s >= 2:
            r = dot(slope_of.pop(s - 2), zf[...]).astype(BF)
            rows[:, rows_of(s - 2), :] = r.reshape(C, G, 4 * K)


def input_gradient(modes, base, zi, yi, wide, spread, out):
    inverse_y(modes, yi, wide, spread)
    for g in range(NG):
        at = rows_of(g)
        v = dot(spread[:, at, :].reshape(C * G, 4 * K), zi[...]) + base[g]
        out[:, at, :] = v.astype(BF).reshape(C, G, COLS)


def point_gradient(g_buf, f_buf, acc, bias_acc, first):
    total, sums = 0.0, 0.0
    for q in range(0, NG, 4):
        gs = [g_buf[:, rows_of(q + e), :].reshape(C * G, COLS) for e in range(4)]
        fs = [f_buf[:, rows_of(q + e), :].reshape(C * G, COLS) for e in range(4)]
        total = total + dot_nt(jnp.concatenate(gs, axis=1), jnp.concatenate(fs, axis=1))
        for gp in gs:
            gp = gp.astype(F32)
            sums = sums + gp[:, : COLS // 2] + gp[:, COLS // 2 :]
    acc[...] = total if first else acc[...] + total
    bias_acc[...] = sums if first else bias_acc[...] + sums


def main_kernel(
    field, cot, weights, zf_all, zi_all, yf_all, yi_all, point, bias, over_o_ref, over_i_ref,
    out, first, base1, modes_out, grad, zi, yi, small_out,
    f_buf, c_buf, spread, rows, g_buf, base0, wide, part, modes, part2, modes2,
    zf, yf, kron, kron_back, bias_col, acc, bias_acc, w_all, spec, dual, s_small, r_small,
    b1, b2, sems, w_sems, small_sems,
):
    at = places()
    gy, gz = lax.axis_index("gy"), lax.axis_index("gz")
    local = pltpu.make_async_copy
    half = C // 2
    loads = [
        local(field.at[:half, 0], f_buf.at[0, :half], sems.at[0]),
        local(zf_all.at[gz], zf, sems.at[1]),
        local(field.at[half:, 0], f_buf.at[0, half:], sems.at[2]),
        local(yf_all.at[gy], yf, sems.at[3]),
        local(field.at[:, 1], f_buf.at[1], sems.at[4]),
        local(weights, w_all.at[at["hi"]], sems.at[5]),
        local(zi_all.at[gz], zi, sems.at[6]),
        local(yi_all.at[gy], yi, sems.at[7]),
        local(cot.at[:, 0], c_buf.at[0], sems.at[8]),
        local(cot.at[:, 1], c_buf.at[1], sems.at[9]),
    ]
    barrier, partners = greet(at)
    for load in loads[:5]:
        load.start()

    loads[0].wait()
    loads[1].wait()
    forward_z(f_buf.at[0], zf, rows.at[0], 0, half)
    loads[2].wait()
    forward_z(f_buf.at[0], zf, rows.at[0], half, C)
    loads[3].wait()
    forward_y(rows.at[0], yf, wide.at[0], part.at[0])
    pl.semaphore_wait(barrier, partners)
    f0 = scatter_core(at, 0, part, b1)
    w_there = pltpu.make_async_remote_copy(
        src_ref=weights,
        dst_ref=w_all.at[at["hi"]],
        send_sem=w_sems.at[0],
        recv_sem=w_sems.at[1],
        device_id=device(at, hi=1 - at["hi"]),
        device_id_type=MESH,
    )
    loads[4].wait()
    forward_z(f_buf.at[1], zf, rows.at[1], 0, C)
    arrived(f0)
    f0 = scatter_rows(at, 0, part, b1)
    forward_y(rows.at[1], yf, wide.at[1], part.at[1])
    f1 = scatter_core(at, 1, part, b1)
    same, over = group_masks()
    kron[...] = kron_of(dot(over, point[...]), over, same)
    bias_wide = jnp.broadcast_to(bias[...].astype(F32), (2 * K, C)).astype(BF)
    bias_col[...] = dot_nt(over, bias_wide)
    over_o, over_i = over_o_ref[...], over_i_ref[...]
    w_there.start()
    for load in loads[5:8]:
        load.start()
    pointwise(f_buf.at[0], kron, bias_col, base0)
    arrived(f0)
    f0 = scatter_halves(at, 0, b1)
    arrived(f1)
    f1 = scatter_rows(at, 1, part, b1)
    for load in loads[8:]:
        load.start()
    pointwise(f_buf.at[1], kron, bias_col, base1)
    for load in loads[5:8]:
        load.wait()
    w_there.wait()
    w = w_all[...].reshape(K, 2 * C * C)
    arrived(f0)
    mix(at, 0, scatter_total(at, 0, b1), w, over_o, over_i, modes, spec)
    f0 = gather_rows(at, 0, modes, b1)
    arrived(f1)
    f1 = scatter_halves(at, 1, b1)
    kron_back[...] = kron_of(dot_nt(over, point[...]), over, same)
    f0 = gather_core(at, 0, modes, b1, f0)
    arrived(f1)
    mix(at, 1, scatter_total(at, 1, b1), w, over_o, over_i, modes, spec)
    f1 = gather_rows(at, 1, modes, b1)

    for load in loads[8:]:
        load.wait()
    arrived(f0)
    inverse_y(modes.at[0], yi, wide.at[0], spread.at[0])
    layer(spread.at[0], base0, c_buf.at[0], zi, zf, out.at[0], g_buf.at[0], rows.at[0])
    forward_y(rows.at[0], yf, wide.at[0], part2.at[0])
    f0 = scatter_core(at, 0, part2, b2)
    f1 = gather_core(at, 1, modes, b1, f1)
    arrived(f0)
    f0 = scatter_rows(at, 0, part2, b2)
    arrived(f1)
    inverse_y(modes.at[1], yi, wide.at[1], spread.at[1])
    layer(spread.at[1], base1, c_buf.at[1], zi, zf, out.at[1], g_buf.at[1], rows.at[1])
    forward_y(rows.at[1], yf, wide.at[1], part2.at[1])
    f1 = scatter_core(at, 1, part2, b2)

    arrived(f1)
    f1 = scatter_rows(at, 1, part2, b2)
    arrived(f0)
    f0 = scatter_halves(at, 0, b2)
    point_gradient(g_buf.at[0], f_buf.at[0], acc, bias_acc, True)
    point_gradient(g_buf.at[1], f_buf.at[1], acc, bias_acc, False)
    same, over = group_masks()
    kept = jnp.where(same, acc[...], 0.0).reshape(C, G, C * G).sum(axis=1)
    term = jnp.dot(kept, over.astype(F32), precision=lax.Precision.HIGHEST)
    total = bias_acc[...].reshape(C, G, COLS // 2).sum(axis=1).sum(axis=1, keepdims=True)
    s_small[0, :8] = fold(term)
    s_small[0, 8:] = fold(jnp.broadcast_to(total, (C, C)))
    small = [
        send(s_small.at[0], r_small.at[n], small_sems, n, to) for n, to in enumerate(across(at))
    ]
    arrived(f0)
    unmix(at, 0, scatter_total(at, 0, b2), w, over_o, over_i, modes2, dual)
    arrived(f1)
    f1 = scatter_halves(at, 1, b2)
    f0 = gather_rows(at, 0, modes2, b2)
    pointwise_back(g_buf.at[0], kron_back, base0)
    arrived(small)
    s_small[1] = s_small[0] + r_small[0] + r_small[1] + r_small[2]
    arrived(f1)
    unmix(at, 1, scatter_total(at, 1, b2), w, over_o, over_i, modes2, dual)
    f1 = gather_rows(at, 1, modes2, b2)
    small = [
        send(s_small.at[1], r_small.at[3 + n], small_sems, 3 + n, device(at, **moved(at, step)))
        for n, step in enumerate(STEPS)
    ]
    weight_gradient(at, spec, dual, over_o, over_i, grad)
    pointwise_back(g_buf.at[1], kron_back, base1)
    f0 = gather_core(at, 0, modes2, b2, f0)
    arrived(f0)
    input_gradient(modes2.at[0], base0, zi, yi, wide.at[0], spread.at[0], first)
    f1 = gather_core(at, 1, modes2, b2, f1)
    arrived(small)
    total = s_small[1]
    for n in range(len(STEPS)):
        total = total + r_small[3 + n]
    small_out[...] = total * (1.0 / math.sqrt(X * Y * Z))
    arrived(f1)
    modes_out[...] = modes2[1]


def last_kernel(
    held, first, base, modes, grad_in, zi, yi, small,
    out, output, grad, term, total, spread, second, wide, out_sems,
):
    local = pltpu.make_async_copy
    outs = [
        local(first, out.at[:, 0], out_sems.at[0]),
        local(held.at[0], output.at[:, 0], out_sems.at[1]),
        local(held.at[1], output.at[:, 1], out_sems.at[2]),
        local(grad_in, grad, out_sems.at[3]),
    ]
    for copy in outs:
        copy.start()
    term[...] = unfold(small[:8])
    total[...] = unfold(small[8:]).T[:1]
    input_gradient(modes, base, zi, yi, wide, spread, second)
    outs.append(local(second, out.at[:, 1], out_sems.at[4]))
    outs[-1].start()
    for copy in outs:
        copy.wait()


VMEM = pl.BlockSpec(memory_space=pltpu.VMEM)
ANY = pl.BlockSpec(memory_space=pl.ANY)


def params(mib, collective_id=None):
    limit = mib * 1024 * 1024
    if collective_id is None:
        return pltpu.CompilerParams(vmem_limit_bytes=limit)
    return pltpu.CompilerParams(
        vmem_limit_bytes=limit, collective_id=collective_id, has_side_effects=True
    )


def grid_buffer(dtype=BF):
    return pltpu.VMEM((X, C, ROWS, COLS), dtype)


def local(field, spec_weight, point_weight, bias, cotangent):
    zf, zi, yf, yi = (jnp.asarray(t) for t in make_tables())
    over_o, over_i = (jnp.asarray(t) for t in make_spreads())
    shape = jax.ShapeDtypeStruct
    deep = (X, 2, 4, 4, 2, C, 2 * K)
    lines = pltpu.VMEM((X, C, ROWS, 4 * K), BF)
    sample = pltpu.VMEM((C, ROWS, COLS), BF)
    rows_wide = pltpu.VMEM((NG, C * G, COLS), F32)
    wide = (K * C, 2 * K)
    table = pltpu.VMEM((COLS, COLS), BF)
    vmem = pltpu.VMEM
    dma = pltpu.SemaphoreType.DMA
    square = (C * G, C * G)

    held, first, base, modes, grad_spec, zi, yi, small = pl.pallas_call(
        main_kernel,
        out_shape=(
            grid_buffer(),
            sample,
            rows_wide,
            vmem(deep[1:], BF),
            vmem((K // 2, 2 * C * C), F32),
            table,
            vmem((2 * ROWS, K), BF),
            vmem((16, 4 * C), F32),
        ),
        in_specs=[ANY] * 7 + [VMEM] * 4,
        out_specs=[VMEM] * 8,
        scratch_shapes=[
            grid_buffer(), grid_buffer(), lines, lines, grid_buffer(), rows_wide,
            vmem((X,) + wide, F32), vmem(deep, BF), vmem(deep, BF), vmem(deep, BF), vmem(deep, BF),
            table, vmem((K, 2 * ROWS), BF),
            vmem(square, BF), vmem(square, BF), vmem((C * G, 2 * K), F32), vmem(square, F32),
            vmem((C * G, COLS // 2), F32),
            vmem((2, K // 2, 2 * C * C), BF),
            vmem((X, 2 * K, C), F32), vmem((X, 2 * K, C), F32),
            vmem((2, 16, 4 * C), F32), vmem((3 + len(STEPS), 16, 4 * C), F32),
            exchange_scratch(), exchange_scratch(),
            dma((10,)), dma((2,)), [dma((3 + len(STEPS),)), dma((3 + len(STEPS),))],
        ],
        compiler_params=params(51, 1),
        name="layer",
    )(
        field, cotangent, spec_weight, zf, zi, yf, yi,
        point_weight, bias.reshape(1, C), over_o, over_i,
    )

    grad_input, output, grad, term, total = pl.pallas_call(
        last_kernel,
        out_shape=(
            shape(field.shape, BF),
            shape(field.shape, BF),
            shape(grad_spec.shape, F32),
            shape((C, C), F32),
            shape((1, C), F32),
        ),
        in_specs=[VMEM] * 8,
        out_specs=[ANY] * 3 + [VMEM] * 2,
        scratch_shapes=[vmem((C, ROWS, 4 * K), BF), sample, vmem(wide, F32), dma((5,))],
        compiler_params=params(24),
        name="input_gradient",
    )(held, first, base, modes, grad_spec, zi, yi, small)

    return output, grad_input, grad, term, total.reshape(C)


def solution(mesh):
    grid = P(None, None, "gy", "gz")
    owned = P(("gy", "gz"), None)
    return jax.shard_map(
        local,
        mesh=mesh,
        in_specs=(grid, owned, P(), P(), grid),
        out_specs=(grid, grid, owned, P(), P()),
        check_vma=False,
    )
```
